32 devices in a mesh: mp: 8 (over y, x, core), replica: 4 (over z).
Axes of the slice: x: 2, y: 2, z: 4, core: 2. Of those that a mesh axis runs over, the one named last changes fastest.
Arguments:
- table: float32 [32768, 128], P('mp'), may hold values from -6 to 6
- accum: float32 [32768, 128], P('mp'), may hold values from 100 to 1000
- lookup_slots: int32 [4096, 32], P('replica', 'mp'), may hold values from 0 to 1023
- lookup_weights: int32 [4096, 32], P('replica', 'mp'), may hold values from 1 to 3
- touched_rows: int32 [8192], P('mp'), may hold values from 0 to 4095, as said below
- pooled_grad: bfloat16 [4096, 128], P(('replica', 'mp')), may hold values from -6 to 6
Outputs:
- pooled: float32 [4096, 128], P(('replica', 'mp'))
- new_table: float32 [32768, 128], P('mp')
- new_accum: float32 [32768, 128], P('mp')
The draws below stay inside these ranges and needn't reach their ends.
Inputs may be any that keep to these rules, and one draw needn't show every extreme that they name: `touched_rows`: within each shard's block of 1024 entries the row ids are distinct.
All inputs are finite; a program needn't handle non-finite values.
Results may differ from the reference program's by a relative error of at most 0.0029.
Values may be sent and summed in bfloat16 or wider, within the bound.
No kernel may reach another device: no remote copies, remote signals or barrier semaphores. Data moves between devices by JAX's collectives and lax.ppermute only.
A program may use at most 64 MiB of HBM per device.

```python
import math
import jax
import jax.numpy as jnp
from jax import lax

E = 128
ROWS_DEV = 4096
N_TOUCH = 1024
HOTS = 4
BAGS = 1024
BAGS_ALL = 4096
ROWS = 32768
N_MP = 8
N_REPLICA = 4


def draw_touched_rows(key, part):
    key = jax.random.fold_in(key, 7)
    shard_keys = jax.random.split(key, N_MP)

    def one_shard(shard_key):
        return jax.random.permutation(shard_key, ROWS_DEV)[:N_TOUCH].astype(jnp.int32)
    return jax.vmap(one_shard)(shard_keys).reshape(N_MP * N_TOUCH)


def plant(array, rng, smallest, largest):
    extent = array.shape
    spot = [jax.random.randint(jax.random.fold_in(rng, axis), (), 0, extent[axis]) for axis in range(len(extent))]
    array = array.at[tuple(spot)].set(smallest)
    longest = extent.index(max(extent))
    spot[longest] = (spot[longest] + 1) % extent[longest]
    return array.at[tuple(spot)].set(largest)


def level_of(rng, dims, cuts, smallest, high):
    def one(dim, parts):
        heights = jax.random.uniform(jax.random.fold_in(jax.random.fold_in(rng, 6), dim), (parts,), jnp.float32, smallest / len(cuts), high / len(cuts))
        return jnp.repeat(jnp.exp(heights), dims[dim] // parts).reshape((-1,) + (1,) * (len(dims) - dim - 1))

    level = one(*cuts[0])
    for cut in cuts[1:]:
        level = level * one(*cut)
    return level


def scatter_about(own_key, extent, deviation, limit, cuts=(), held_as=jnp.bfloat16):
    drawn = deviation * jax.random.normal(own_key, extent, jnp.float32)
    if cuts:
        drawn = drawn * level_of(own_key, extent, cuts, -0.22, 0.18)
    return jnp.clip(drawn, -limit, limit).astype(held_as)


def setup_inputs(seed: int = 0) -> dict:
    key_list = jax.random.split(jax.random.key(seed), 7)
    return {
        "table": scatter_about(key_list[0], (ROWS, E), 1.0, 6.0, ((0, 8),), jnp.float32),
        "accum": jnp.clip(jnp.exp(math.log(1000.0) - 2.3025851 * jax.random.uniform(key_list[1], (ROWS, E), jnp.float32) ** level_of(key_list[1], (ROWS, E), ((0, 8),), -0.2, 0.2)), 100.0, 1000.0),
        "lookup_slots": plant(jax.random.randint(key_list[2], (BAGS_ALL, N_MP * HOTS), 0, N_TOUCH), jax.random.fold_in(key_list[2], 1), 0, N_TOUCH - 1).astype(jnp.int32),
        "lookup_weights": plant(jax.random.randint(key_list[3], (BAGS_ALL, N_MP * HOTS), 1, 4), jax.random.fold_in(key_list[3], 1), 1, 3).astype(jnp.int32),
        "touched_rows": draw_touched_rows(jax.random.fold_in(key_list[6], 71), 0),
        "pooled_grad": scatter_about(key_list[5], (BAGS_ALL, E), 1.0, 6.0, ((0, 32),)),
    }


learn_rate = 0.5

def reference(table, accum, lookup_slots, lookup_weights, touched_rows, pooled_grad):
    tables = table.reshape(N_MP, ROWS_DEV, E)
    histories = accum.reshape(N_MP, ROWS_DEV, E)
    slot_all = lookup_slots.reshape(N_REPLICA, BAGS, N_MP, HOTS)
    weight_all = lookup_weights.reshape(N_REPLICA, BAGS, N_MP, HOTS).astype(jnp.float32)
    rows_all = touched_rows.reshape(N_MP, N_TOUCH)
    grads = pooled_grad.reshape(N_REPLICA, BAGS, E).astype(jnp.float32)

    def shard_step(pooled_sum, shard):
        rows_here = rows_all[shard]
        row_values = tables[shard][rows_here]
        low_values = lax.optimization_barrier(row_values.astype(jnp.bfloat16)).astype(jnp.float32)
        slot_here = slot_all[:, :, shard, :]
        weight_here = weight_all[:, :, shard, :]
        gathered = low_values[slot_here]
        partial_value = lax.optimization_barrier(jnp.sum(weight_here[..., None] * gathered, axis=2))
        contrib = weight_here[..., None] * grads[:, :, None, :]
        gradient = jnp.zeros((N_TOUCH, E), jnp.float32).at[slot_here.reshape(-1)].add(contrib.reshape(-1, E))
        history_new = histories[shard][rows_here] + gradient * gradient
        updated = row_values - learn_rate * gradient / jnp.sqrt(history_new)
        return (pooled_sum + partial_value, (updated, history_new))
    start_sum = jnp.zeros((N_REPLICA, BAGS, E), jnp.float32)
    pooled_sum, (updated, history_new) = lax.scan(shard_step, start_sum, jnp.arange(N_MP, dtype=jnp.int32))
    shard_ids = jnp.arange(N_MP, dtype=jnp.int32)[:, None]
    new_tables = tables.at[shard_ids, rows_all].set(updated)
    new_histories = histories.at[shard_ids, rows_all].set(history_new)
    return (pooled_sum.reshape(N_REPLICA * BAGS, E), new_tables.reshape(ROWS, E), new_histories.reshape(ROWS, E))
```

```python
import functools
import math

import jax
import jax.numpy as jnp
from jax import lax
from jax.experimental import pallas as pl
from jax.experimental.pallas import tpu as pltpu
from jax.sharding import PartitionSpec as P

learn_rate = 0.5
LANES = 128
MIB = 1 << 20


def build_counts(slots, weights, touch_count):
    bag_count = slots.shape[0]
    block_rows = math.gcd(bag_count, 512)
    columns = jnp.arange(touch_count, dtype=jnp.int32)

    def one_block(block_index):
        slot_block = lax.dynamic_slice_in_dim(slots, block_index * block_rows, block_rows, 0)
        weight_block = lax.dynamic_slice_in_dim(weights, block_index * block_rows, block_rows, 0)
        matches = (slot_block[:, :, None] == columns[None, None, :]).astype(jnp.float32)
        return jnp.sum(matches * weight_block[:, :, None].astype(jnp.float32), axis=1).astype(
            jnp.bfloat16
        )

    blocks = lax.map(one_block, jnp.arange(bag_count // block_rows, dtype=jnp.int32))
    return blocks.reshape(bag_count, touch_count)


def adagrad(row_values, history, gradient):
    history_new = history + gradient * gradient
    return (row_values - learn_rate * gradient / jnp.sqrt(history_new), history_new)


def per_device_general(table, accum, lookup_slots, lookup_weights, touched_rows, pooled_grad):
    touch_count = touched_rows.shape[0]
    feature_dim = table.shape[1]
    bag_local = pooled_grad.shape[0]
    mp_count = lax.axis_size("mp")
    counts = build_counts(lookup_slots, lookup_weights, touch_count)
    row_tile = table[touched_rows]
    tile_low = row_tile.astype(jnp.bfloat16)
    partial_value = jnp.dot(counts, tile_low, preferred_element_type=jnp.float32)
    received = lax.all_to_all(
        partial_value.reshape(mp_count, bag_local, feature_dim),
        "mp",
        split_axis=0,
        concat_axis=0,
        tiled=True,
    )
    pooled = jnp.sum(received, axis=0)
    local_grad = lax.dot_general(
        counts,
        lax.all_gather(pooled_grad, "mp", axis=0, tiled=True),
        (((0,), (0,)), ((), ())),
        preferred_element_type=jnp.float32,
    )
    gradient = lax.psum(local_grad.astype(jnp.bfloat16), "replica").astype(jnp.float32)
    new_rows, new_history = adagrad(row_tile, accum[touched_rows], gradient)
    new_table = table.at[touched_rows].set(new_rows)
    new_accum = accum.at[touched_rows].set(new_history)
    return (pooled, new_table, new_accum)


def vmem():
    return pl.BlockSpec(memory_space=pltpu.VMEM)


def smem():
    return pl.BlockSpec(memory_space=pltpu.SMEM)


def anywhere():
    return pl.BlockSpec(memory_space=pl.ANY)


def params(mib):
    return pltpu.CompilerParams(vmem_limit_bytes=mib * MIB)


def pack_kernel(grad_ref, slots_ref, weights_ref, out_ref, slot_rows, weight_rows):
    hots, bags = slots_ref.shape
    rows = grad_ref.shape[0]
    blocks = bags // LANES
    out_ref[pl.ds(0, rows), :] = grad_ref[...]
    for h in range(hots):
        for j in range(blocks):
            slot_rows[pl.ds(h * blocks + j, 1), :] = slots_ref[pl.ds(h, 1), pl.ds(j * LANES, LANES)]
            weight_rows[pl.ds(h * blocks + j, 1), :] = weights_ref[pl.ds(h, 1), pl.ds(j * LANES, LANES)]
    slot = slot_rows[...]
    code = weight_rows[...] * 64 + lax.shift_right_logical(slot, 8)
    low = jnp.bitwise_and(slot, 255)
    lookups = hots * blocks
    out_ref[pl.ds(rows, lookups), :] = low.astype(jnp.float32).astype(jnp.bfloat16)
    out_ref[pl.ds(rows + lookups, lookups), :] = code.astype(jnp.float32).astype(jnp.bfloat16)


def fill_counts(packed_ref, rows, hots, blocks, touch, low_rows, code_rows, write):
    lookups = hots * blocks
    low_rows[...] = packed_ref[pl.ds(rows, lookups), :].astype(jnp.float32)
    code_rows[...] = packed_ref[pl.ds(rows + lookups, lookups), :].astype(jnp.float32)
    step = min(touch, 256)
    line = lax.broadcasted_iota(jnp.int32, (step, LANES), 0).astype(jnp.float32).astype(jnp.bfloat16)
    zero = jnp.zeros((step, LANES), jnp.bfloat16)

    def one(j, carry):
        lows, highs, weights = [], [], []
        for h in range(hots):
            low = low_rows[pl.ds(h * blocks + j, 1), :]
            code = code_rows[pl.ds(h * blocks + j, 1), :].astype(jnp.int32)
            lows.append(low)
            highs.append(jnp.bitwise_and(code, 63))
            weights.append(lax.shift_right_logical(code, 6).astype(jnp.float32).astype(jnp.bfloat16))
        for k in range(touch // step):
            total = None
            for h in range(hots):
                at = jnp.where(highs[h] == k, lows[h], -1.0).astype(jnp.bfloat16)
                at = jnp.broadcast_to(at, (step, LANES))
                term = jnp.where(at == line, jnp.broadcast_to(weights[h], (step, LANES)), zero)
                total = term if total is None else total + term
            write(j, k, total)
        return carry

    lax.fori_loop(0, blocks, one, 0)


def pooled_kernel(hots, mp, touched_ref, packed_ref, table_ref, keep_ref, send_ref, counts_ref,
                  table_vmem, tile, low_rows, code_rows, sum_t, sem):
    touch = touched_ref.shape[0]
    bags = counts_ref.shape[1]
    rows = bags // mp
    blocks = bags // LANES
    me = lax.axis_index("mp")
    copy = pltpu.make_async_copy(table_ref, table_vmem, sem)
    copy.start()

    def write(j, k, block):
        counts_ref[pl.ds(k * block.shape[0], block.shape[0]),
                   pl.ds(pl.multiple_of(j * LANES, LANES), LANES)] = block

    fill_counts(packed_ref, rows, hots, blocks, touch, low_rows, code_rows, write)
    copy.wait()

    def gather(i, carry):
        for u in range(16):
            t = i * 16 + u
            tile[pl.ds(t, 1), :] = table_vmem[pl.ds(touched_ref[t], 1), :]
        return carry

    lax.fori_loop(0, touch // 16, gather, 0)
    tile_t = tile[...].T.astype(jnp.bfloat16)
    sum_t[...] = jnp.dot(tile_t, counts_ref[...], preferred_element_type=jnp.float32)
    for c in range(mp // 2):
        for odd, ref in ((0, keep_ref), (1, send_ref)):
            owner = jnp.bitwise_xor(me, 2 * c + odd)
            block = sum_t[:, pl.ds(pl.multiple_of(owner * rows, rows), rows)]
            ref[c] = block.T


def join_kernel(rows, *refs):
    out_ref = refs[-1]
    for d, ref in enumerate(refs[:-1]):
        out_ref[pl.ds(d * rows, rows), :] = ref[pl.ds(0, rows), :]


def counts_kernel(hots, rows, *refs):
    peers, counts_ref, low_rows, code_rows = refs[:-3], refs[-3], refs[-2], refs[-1]
    touch = counts_ref.shape[0]
    bags = counts_ref.shape[1] // len(peers)
    for d, ref in enumerate(peers):

        def write(j, k, block, d=d):
            counts_ref[pl.ds(k * block.shape[0], block.shape[0]),
                       pl.ds(pl.multiple_of(d * bags + j * LANES, LANES), LANES)] = block

        fill_counts(ref, rows, hots, bags // LANES, touch, low_rows, code_rows, write)


def update_kernel(mp, replicas, rows, touched_ref, own_ref, rest_ref, *refs):
    blocks = refs[:mp]
    table_ref, accum_ref, new_table_ref, new_accum_ref = refs[mp:mp + 4]
    grads, summed, full, table_vmem, accum_vmem, in_sem, out_sem = refs[mp + 4:]
    touch = touched_ref.shape[0]
    total_rows = full.shape[0]
    bags = mp * rows
    me = lax.axis_index("mp")
    loads = [
        pltpu.make_async_copy(table_ref, table_vmem, in_sem.at[0]),
        pltpu.make_async_copy(accum_ref, accum_vmem, in_sem.at[1]),
    ]
    for load in loads:
        load.start()
    full[...] = jnp.zeros_like(full)
    for m, ref in enumerate(blocks):
        owner = jnp.bitwise_xor(me, m)
        for d in range(replicas):
            place = pl.multiple_of(d * bags + owner * rows, rows)
            grads[pl.ds(place, rows), :] = ref[pl.ds(d * rows, rows), :]
    gradient = jnp.dot(own_ref[...], grads[pl.ds(0, bags), :], preferred_element_type=jnp.float32)
    gradient += jnp.dot(
        rest_ref[...], grads[pl.ds(bags, bags * (replicas - 1)), :], preferred_element_type=jnp.float32
    )
    summed[...] = gradient

    def scatter(i, carry):
        for u in range(16):
            t = i * 16 + u
            full[pl.ds(touched_ref[t], 1), :] = summed[pl.ds(t, 1), :]
        return carry

    lax.fori_loop(0, touch // 16, scatter, 0)
    for load in loads:
        load.wait()
    chunks = 8
    size = total_rows // chunks
    stores = []
    for c in range(chunks):
        part = pl.ds(c * size, size)
        change = full[part, :]
        history = accum_vmem[part, :] + change * change
        table_vmem[part, :] = table_vmem[part, :] - learn_rate * change * lax.rsqrt(history)
        accum_vmem[part, :] = history
        for held, out, s in ((table_vmem, new_table_ref, 0), (accum_vmem, new_accum_ref, 1)):
            store = pltpu.make_async_copy(held.at[part, :], out.at[part, :], out_sem.at[s, c])
            store.start()
            stores.append(store)
    for store in stores:
        store.wait()


def per_device_small(table, accum, lookup_slots, lookup_weights, touched_rows, pooled_grad):
    bags, hots = lookup_slots.shape
    touch = touched_rows.shape[0]
    rows, feature = pooled_grad.shape
    table_rows = table.shape[0]
    mp = lax.axis_size("mp")
    replicas = lax.axis_size("replica")
    lookups = hots * (bags // LANES)
    low = jnp.bfloat16

    def swap(value, axis, distance):
        return lax.ppermute(value, axis, [(i, i ^ distance) for i in range(lax.axis_size(axis))])

    packed = pl.pallas_call(
        pack_kernel,
        out_shape=jax.ShapeDtypeStruct((rows + 2 * lookups, LANES), low),
        in_specs=[vmem(), vmem(), vmem()],
        out_specs=vmem(),
        scratch_shapes=[pltpu.VMEM((lookups, LANES), jnp.int32)] * 2,
        compiler_params=params(8),
        name="pack",
    )(pooled_grad, lookup_slots.T, lookup_weights.T)
    peers = [swap(packed, "replica", d) for d in range(1, replicas)]

    keep, send, own_counts = pl.pallas_call(
        functools.partial(pooled_kernel, hots, mp),
        out_shape=[
            jax.ShapeDtypeStruct((mp // 2, rows, feature), jnp.float32),
            jax.ShapeDtypeStruct((mp // 2, rows, feature), jnp.float32),
            jax.ShapeDtypeStruct((touch, bags), low),
        ],
        in_specs=[smem(), vmem(), anywhere()],
        out_specs=[vmem(), vmem(), vmem()],
        scratch_shapes=[
            pltpu.VMEM((table_rows, feature), jnp.float32),
            pltpu.VMEM((touch, feature), jnp.float32),
            pltpu.VMEM((lookups, LANES), jnp.float32),
            pltpu.VMEM((lookups, LANES), jnp.float32),
            pltpu.VMEM((feature, bags), jnp.float32),
            pltpu.SemaphoreType.DMA,
        ],
        compiler_params=params(20),
        cost_estimate=pl.CostEstimate(flops=2 * touch * bags * feature, bytes_accessed=8 * MIB, transcendentals=0),
        name="pool",
    )(touched_rows, packed, table)
    halves = keep + swap(send, "mp", 1)

    joined = pl.pallas_call(
        functools.partial(join_kernel, rows),
        out_shape=jax.ShapeDtypeStruct((replicas * rows, feature), low),
        in_specs=[vmem()] * replicas,
        out_specs=vmem(),
        compiler_params=params(8),
        name="join",
    )(packed, *peers)
    far = [swap(joined, "mp", 2 * c) for c in range(1, mp // 2)]
    same = [joined] + far
    other = [swap(value, "mp", 1) for value in same]
    blocks = [value for pair in zip(same, other) for value in pair]

    pooled = halves[0]
    for c in range(1, mp // 2):
        pooled = pooled + swap(halves[c], "mp", 2 * c)

    rest_counts = pl.pallas_call(
        functools.partial(counts_kernel, hots, rows),
        out_shape=jax.ShapeDtypeStruct((touch, bags * (replicas - 1)), low),
        in_specs=[vmem()] * (replicas - 1),
        out_specs=vmem(),
        scratch_shapes=[pltpu.VMEM((lookups, LANES), jnp.float32)] * 2,
        compiler_params=params(16),
        cost_estimate=pl.CostEstimate(flops=0, bytes_accessed=12 * MIB, transcendentals=0),
        name="count",
    )(*peers)

    new_table, new_accum = pl.pallas_call(
        functools.partial(update_kernel, mp, replicas, rows),
        out_shape=[jax.ShapeDtypeStruct(table.shape, jnp.float32)] * 2,
        in_specs=[smem()] + [vmem()] * (2 + mp) + [anywhere()] * 2,
        out_specs=[anywhere()] * 2,
        scratch_shapes=[
            pltpu.VMEM((bags * replicas, feature), low),
            pltpu.VMEM((touch, feature), jnp.float32),
            pltpu.VMEM((table_rows, feature), jnp.float32),
            pltpu.VMEM((table_rows, feature), jnp.float32),
            pltpu.VMEM((table_rows, feature), jnp.float32),
            pltpu.SemaphoreType.DMA((2,)),
            pltpu.SemaphoreType.DMA((2, 8)),
        ],
        compiler_params=params(32),
        cost_estimate=pl.CostEstimate(
            flops=2 * touch * bags * replicas * feature, bytes_accessed=16 * MIB, transcendentals=0
        ),
        name="update",
    )(touched_rows, own_counts, rest_counts, *blocks, table, accum)
    return (pooled, new_table, new_accum)


def fits_small(mesh, table, lookup_slots, touched_rows, pooled_grad):
    mp, replicas = mesh.shape["mp"], mesh.shape["replica"]
    powers = all(n >= 2 and n & (n - 1) == 0 for n in (mp, replicas))
    touch = touched_rows.shape[0] // mp
    bags = lookup_slots.shape[0] // replicas
    rows = pooled_grad.shape[0] // (mp * replicas)
    return (
        powers
        and mp <= 8
        and replicas <= 4
        and lookup_slots.shape[0] * touch <= 4096 * 1024
        and touch % 256 == 0
        and touch <= 16384
        and bags % LANES == 0
        and rows % LANES == 0
        and table.shape[1] == LANES
        and table.shape[0] // mp <= 4096
        and table.shape[0] // mp % 64 == 0
    )


def solution(mesh):
    placed = (
        P("mp", None),
        P("mp", None),
        P("replica", "mp"),
        P("replica", "mp"),
        P("mp"),
        P(("replica", "mp"), None),
    )

    def step(table, accum, lookup_slots, lookup_weights, touched_rows, pooled_grad):
        small = fits_small(mesh, table, lookup_slots, touched_rows, pooled_grad)
        return jax.shard_map(
            per_device_small if small else per_device_general,
            mesh=mesh,
            in_specs=placed,
            out_specs=(P(("replica", "mp"), None), P("mp", None), P("mp", None)),
            check_vma=False,
        )(table, accum, lookup_slots, lookup_weights, touched_rows, pooled_grad)

    return step
```

```python
import functools
import math

import jax
import jax.numpy as jnp
from jax import lax
from jax.experimental import pallas as pl
from jax.experimental.pallas import tpu as pltpu
from jax.sharding import PartitionSpec as P

learn_rate = 0.5
LANES = 128
MIB = 1 << 20


def build_counts(slots, weights, touch_count):
    bag_count = slots.shape[0]
    block_rows = math.gcd(bag_count, 512)
    columns = jnp.arange(touch_count, dtype=jnp.int32)

    def one_block(block_index):
        slot_block = lax.dynamic_slice_in_dim(slots, block_index * block_rows, block_rows, 0)
        weight_block = lax.dynamic_slice_in_dim(weights, block_index * block_rows, block_rows, 0)
        matches = (slot_block[:, :, None] == columns[None, None, :]).astype(jnp.float32)
        return jnp.sum(matches * weight_block[:, :, None].astype(jnp.float32), axis=1).astype(
            jnp.bfloat16
        )

    blocks = lax.map(one_block, jnp.arange(bag_count // block_rows, dtype=jnp.int32))
    return blocks.reshape(bag_count, touch_count)


def adagrad(row_values, history, gradient):
    history_new = history + gradient * gradient
    return (row_values - learn_rate * gradient / jnp.sqrt(history_new), history_new)


def per_device_general(table, accum, lookup_slots, lookup_weights, touched_rows, pooled_grad):
    touch_count = touched_rows.shape[0]
    feature_dim = table.shape[1]
    bag_local = pooled_grad.shape[0]
    mp_count = lax.axis_size("mp")
    counts = build_counts(lookup_slots, lookup_weights, touch_count)
    row_tile = table[touched_rows]
    tile_low = row_tile.astype(jnp.bfloat16)
    partial_value = jnp.dot(counts, tile_low, preferred_element_type=jnp.float32)
    received = lax.all_to_all(
        partial_value.reshape(mp_count, bag_local, feature_dim),
        "mp",
        split_axis=0,
        concat_axis=0,
        tiled=True,
    )
    pooled = jnp.sum(received, axis=0)
    local_grad = lax.dot_general(
        counts,
        lax.all_gather(pooled_grad, "mp", axis=0, tiled=True),
        (((0,), (0,)), ((), ())),
        preferred_element_type=jnp.float32,
    )
    gradient = lax.psum(local_grad.astype(jnp.bfloat16), "replica").astype(jnp.float32)
    new_rows, new_history = adagrad(row_tile, accum[touched_rows], gradient)
    new_table = table.at[touched_rows].set(new_rows)
    new_accum = accum.at[touched_rows].set(new_history)
    return (pooled, new_table, new_accum)


def vmem():
    return pl.BlockSpec(memory_space=pltpu.VMEM)


def smem():
    return pl.BlockSpec(memory_space=pltpu.SMEM)


def hbm():
    return pl.BlockSpec(memory_space=pltpu.HBM)


def in_hbm(value):
    return pltpu.with_memory_space_constraint(value, pltpu.HBM)


def params(mib):
    return pltpu.CompilerParams(vmem_limit_bytes=mib * MIB)


def pack_kernel(grad_hbm, slots_hbm, weights_hbm, out_ref, slots_ref, weights_ref, slot_rows, weight_rows, sem):
    hots, bags = slots_ref.shape
    rows = grad_hbm.shape[0]
    blocks = bags // LANES
    loads = [
        pltpu.make_async_copy(slots_hbm, slots_ref, sem.at[0]),
        pltpu.make_async_copy(weights_hbm, weights_ref, sem.at[1]),
        pltpu.make_async_copy(grad_hbm, out_ref.at[pl.ds(0, rows), :], sem.at[2]),
    ]
    for load in loads:
        load.start()
    for load in loads:
        load.wait()
    for h in range(hots):
        for j in range(blocks):
            slot_rows[pl.ds(h * blocks + j, 1), :] = slots_ref[pl.ds(h, 1), pl.ds(j * LANES, LANES)]
            weight_rows[pl.ds(h * blocks + j, 1), :] = weights_ref[pl.ds(h, 1), pl.ds(j * LANES, LANES)]
    slot = slot_rows[...]
    code = weight_rows[...] * 64 + lax.shift_right_logical(slot, 8)
    low = jnp.bitwise_and(slot, 255)
    lookups = hots * blocks
    out_ref[pl.ds(rows, lookups), :] = low.astype(jnp.float32).astype(jnp.bfloat16)
    out_ref[pl.ds(rows + lookups, lookups), :] = code.astype(jnp.float32).astype(jnp.bfloat16)


def fill_counts(packed_ref, rows, hots, blocks, touch, low_rows, code_rows, write):
    lookups = hots * blocks
    low_rows[...] = packed_ref[pl.ds(rows, lookups), :].astype(jnp.float32)
    code_rows[...] = packed_ref[pl.ds(rows + lookups, lookups), :].astype(jnp.float32)
    step = min(touch, 256)
    line = lax.broadcasted_iota(jnp.int32, (step, LANES), 0).astype(jnp.float32).astype(jnp.bfloat16)
    zero = jnp.zeros((step, LANES), jnp.bfloat16)

    def one(j, carry):
        lows, highs, weights = [], [], []
        for h in range(hots):
            low = low_rows[pl.ds(h * blocks + j, 1), :]
            code = code_rows[pl.ds(h * blocks + j, 1), :].astype(jnp.int32)
            lows.append(low)
            highs.append(jnp.bitwise_and(code, 63))
            weights.append(lax.shift_right_logical(code, 6).astype(jnp.float32).astype(jnp.bfloat16))
        for k in range(touch // step):
            total = None
            for h in range(hots):
                at = jnp.where(highs[h] == k, lows[h], -1.0).astype(jnp.bfloat16)
                at = jnp.broadcast_to(at, (step, LANES))
                term = jnp.where(at == line, jnp.broadcast_to(weights[h], (step, LANES)), zero)
                total = term if total is None else total + term
            write(j, k, total)
        return carry

    lax.fori_loop(0, blocks, one, 0)


def pooled_kernel(hots, mp, touched_hbm, packed_ref, peer_ref, table_hbm, keep_ref, send_ref, counts_ref,
                  table_vmem, tile, low_rows, code_rows, sum_t, touched_ref, sem):
    touch = touched_ref.shape[0]
    bags = counts_ref.shape[1] // 2
    rows = bags // mp
    blocks = bags // LANES
    me = lax.axis_index("mp")
    loads = [
        pltpu.make_async_copy(touched_hbm, touched_ref, sem.at[0]),
        pltpu.make_async_copy(table_hbm, table_vmem, sem.at[1]),
    ]
    for load in loads:
        load.start()

    for d, ref in enumerate((packed_ref, peer_ref)):

        def write(j, k, block, d=d):
            counts_ref[pl.ds(k * block.shape[0], block.shape[0]),
                       pl.ds(pl.multiple_of(d * bags + j * LANES, LANES), LANES)] = block

        fill_counts(ref, rows, hots, blocks, touch, low_rows, code_rows, write)
    for load in loads:
        load.wait()

    def gather(i, carry):
        for u in range(16):
            t = i * 16 + u
            tile[pl.ds(t, 1), :] = table_vmem[pl.ds(touched_ref[t], 1), :]
        return carry

    lax.fori_loop(0, touch // 16, gather, 0)
    tile_t = tile[...].T.astype(jnp.bfloat16)
    sum_t[...] = jnp.dot(tile_t, counts_ref[:, pl.ds(0, bags)], preferred_element_type=jnp.float32)
    for c in range(mp // 2):
        for odd, ref in ((0, keep_ref), (1, send_ref)):
            owner = jnp.bitwise_xor(me, 2 * c + odd)
            block = sum_t[:, pl.ds(pl.multiple_of(owner * rows, rows), rows)]
            ref[c] = block.T


def join_kernel(rows, *refs):
    out_ref = refs[-1]
    for d, ref in enumerate(refs[:-1]):
        out_ref[pl.ds(d * rows, rows), :] = ref[pl.ds(0, rows), :]


def counts_kernel(hots, rows, *refs):
    peers, counts_ref, low_rows, code_rows = refs[:-3], refs[-3], refs[-2], refs[-1]
    touch = counts_ref.shape[0]
    bags = counts_ref.shape[1] // len(peers)
    for d, ref in enumerate(peers):

        def write(j, k, block, d=d):
            counts_ref[pl.ds(k * block.shape[0], block.shape[0]),
                       pl.ds(pl.multiple_of(d * bags + j * LANES, LANES), LANES)] = block

        fill_counts(ref, rows, hots, bags // LANES, touch, low_rows, code_rows, write)


def halves_kernel(keep_ref, got_ref, *outs):
    for c, out_ref in enumerate(outs):
        out_ref[...] = keep_ref[c] + got_ref[c]


def grad_kernel(mp, replicas, rows, near_ref, rest_ref, *refs):
    blocks, sum_ref = refs[:mp], refs[mp]
    grads = refs[mp + 1]
    bags = mp * rows
    me = lax.axis_index("mp")
    for m, ref in enumerate(blocks):
        owner = jnp.bitwise_xor(me, m)
        for d in range(replicas):
            place = pl.multiple_of(d * bags + owner * rows, rows)
            grads[pl.ds(place, rows), :] = ref[pl.ds(d * rows, rows), :]
    near = near_ref.shape[1]
    total = jnp.dot(near_ref[...], grads[pl.ds(0, near), :], preferred_element_type=jnp.float32)
    total += jnp.dot(rest_ref[...], grads[pl.ds(near, rest_ref.shape[1]), :], preferred_element_type=jnp.float32)
    sum_ref[...] = total


def update_kernel(parts, touched_ref, summed, table_ref, accum_ref, *refs):
    pooled_parts = refs[:parts]
    new_table_ref, new_accum_ref, pooled_ref, full, table_vmem, accum_vmem, out_sem = refs[parts:]
    touch = touched_ref.shape[0]
    total_rows = full.shape[0]
    full[...] = jnp.zeros_like(full)

    def scatter(i, carry):
        for u in range(16):
            t = i * 16 + u
            full[pl.ds(touched_ref[t], 1), :] = summed[pl.ds(t, 1), :]
        return carry

    lax.fori_loop(0, touch // 16, scatter, 0)
    chunks = 8
    size = total_rows // chunks
    stores = []
    for c in range(chunks):
        part = pl.ds(c * size, size)
        change = full[part, :]
        history = accum_ref[part, :] + change * change
        table_vmem[part, :] = table_ref[part, :] - learn_rate * change * lax.rsqrt(history)
        accum_vmem[part, :] = history
        for held, out, s in ((table_vmem, new_table_ref, 0), (accum_vmem, new_accum_ref, 1)):
            store = pltpu.make_async_copy(held.at[part, :], out.at[part, :], out_sem.at[s, c])
            store.start()
            stores.append(store)
    pooled = pooled_parts[0][...]
    for part in pooled_parts[1:]:
        pooled = pooled + part[...]
    pooled_ref[...] = pooled
    for store in stores:
        store.wait()


def per_device_small(table, accum, lookup_slots, lookup_weights, touched_rows, pooled_grad):
    bags, hots = lookup_slots.shape
    touch = touched_rows.shape[0]
    rows, feature = pooled_grad.shape
    table_rows = table.shape[0]
    mp = lax.axis_size("mp")
    replicas = lax.axis_size("replica")
    lookups = hots * (bags // LANES)
    low = jnp.bfloat16

    def swap(value, axis, distance):
        return lax.ppermute(value, axis, [(i, i ^ distance) for i in range(lax.axis_size(axis))])

    packed = pl.pallas_call(
        pack_kernel,
        out_shape=jax.ShapeDtypeStruct((rows + 2 * lookups, LANES), low),
        in_specs=[hbm()] * 3,
        out_specs=vmem(),
        scratch_shapes=[pltpu.VMEM((hots, bags), jnp.int32)] * 2
        + [pltpu.VMEM((lookups, LANES), jnp.int32)] * 2
        + [pltpu.SemaphoreType.DMA((3,))],
        compiler_params=params(8),
        name="pack",
    )(in_hbm(pooled_grad), in_hbm(lookup_slots.T), in_hbm(lookup_weights.T))
    peers = [swap(packed, "replica", d) for d in range(1, replicas)]

    keep, send, near_counts = pl.pallas_call(
        functools.partial(pooled_kernel, hots, mp),
        out_shape=[
            jax.ShapeDtypeStruct((mp // 2, rows, feature), jnp.float32),
            jax.ShapeDtypeStruct((mp // 2, rows, feature), jnp.float32),
            jax.ShapeDtypeStruct((touch, 2 * bags), low),
        ],
        in_specs=[hbm(), vmem(), vmem(), hbm()],
        out_specs=[vmem(), vmem(), vmem()],
        scratch_shapes=[
            pltpu.VMEM((table_rows, feature), jnp.float32),
            pltpu.VMEM((touch, feature), jnp.float32),
            pltpu.VMEM((lookups, LANES), jnp.float32),
            pltpu.VMEM((lookups, LANES), jnp.float32),
            pltpu.VMEM((feature, bags), jnp.float32),
            pltpu.SMEM((touch,), jnp.int32),
            pltpu.SemaphoreType.DMA((2,)),
        ],
        compiler_params=params(20),
        cost_estimate=pl.CostEstimate(flops=2 * touch * bags * feature, bytes_accessed=8 * MIB, transcendentals=0),
        name="pool",
    )(in_hbm(touched_rows), packed, peers[0], in_hbm(table))
    got = swap(send, "mp", 1)

    joined = pl.pallas_call(
        functools.partial(join_kernel, rows),
        out_shape=jax.ShapeDtypeStruct((replicas * rows, feature), low),
        in_specs=[vmem()] * replicas,
        out_specs=vmem(),
        compiler_params=params(8),
        name="join",
    )(packed, *peers)
    far = [swap(joined, "mp", 2 * c) for c in range(1, mp // 2)]
    same = [joined] + far
    other = [swap(value, "mp", 1) for value in same]
    blocks = [value for pair in zip(same, other) for value in pair]

    halves = pl.pallas_call(
        halves_kernel,
        out_shape=[jax.ShapeDtypeStruct((rows, feature), jnp.float32)] * (mp // 2),
        in_specs=[vmem()] * 2,
        out_specs=[vmem()] * (mp // 2),
        compiler_params=params(8),
        name="halves",
    )(keep, got)
    pooled_parts = [halves[0]] + [swap(halves[c], "mp", 2 * c) for c in range(1, mp // 2)]

    rest_counts = pl.pallas_call(
        functools.partial(counts_kernel, hots, rows),
        out_shape=jax.ShapeDtypeStruct((touch, bags * (replicas - 2)), low),
        in_specs=[vmem()] * (replicas - 2),
        out_specs=vmem(),
        scratch_shapes=[pltpu.VMEM((lookups, LANES), jnp.float32)] * 2,
        compiler_params=params(16),
        cost_estimate=pl.CostEstimate(flops=0, bytes_accessed=8 * MIB, transcendentals=0),
        name="count",
    )(*peers[1:])

    gradient = pl.pallas_call(
        functools.partial(grad_kernel, mp, replicas, rows),
        out_shape=jax.ShapeDtypeStruct((touch, feature), jnp.float32),
        in_specs=[vmem()] * (2 + mp),
        out_specs=vmem(),
        scratch_shapes=[pltpu.VMEM((bags * replicas, feature), low)],
        compiler_params=params(24),
        cost_estimate=pl.CostEstimate(flops=0, bytes_accessed=MIB, transcendentals=0),
        name="gradient",
    )(near_counts, rest_counts, *blocks)

    new_table, new_accum, pooled = pl.pallas_call(
        functools.partial(update_kernel, len(pooled_parts)),
        out_shape=[jax.ShapeDtypeStruct(table.shape, jnp.float32)] * 2
        + [jax.ShapeDtypeStruct((rows, feature), jnp.float32)],
        in_specs=[smem()] + [vmem()] * (3 + len(pooled_parts)),
        out_specs=[hbm()] * 2 + [vmem()],
        scratch_shapes=[
            pltpu.VMEM((table_rows, feature), jnp.float32),
            pltpu.VMEM((table_rows, feature), jnp.float32),
            pltpu.VMEM((table_rows, feature), jnp.float32),
            pltpu.SemaphoreType.DMA((2, 8)),
        ],
        compiler_params=params(24),
        cost_estimate=pl.CostEstimate(flops=0, bytes_accessed=MIB, transcendentals=0),
        name="update",
    )(touched_rows, gradient, table, accum, *pooled_parts)
    return (pooled, new_table, new_accum)


def fits_small(mesh, table, lookup_slots, touched_rows, pooled_grad):
    mp, replicas = mesh.shape["mp"], mesh.shape["replica"]
    powers = all(n & (n - 1) == 0 for n in (mp, replicas))
    touch = touched_rows.shape[0] // mp
    bags = lookup_slots.shape[0] // replicas
    rows = pooled_grad.shape[0] // (mp * replicas)
    return (
        powers
        and 2 <= mp <= 8
        and replicas == 4
        and lookup_slots.shape[0] * touch <= 4096 * 1024
        and touch % 256 == 0
        and touch <= 16384
        and bags % LANES == 0
        and rows % LANES == 0
        and table.shape[1] == LANES
        and table.shape[0] // mp <= 4096
        and table.shape[0] // mp % 64 == 0
    )


def solution(mesh):
    placed = (
        P("mp", None),
        P("mp", None),
        P("replica", "mp"),
        P("replica", "mp"),
        P("mp"),
        P(("replica", "mp"), None),
    )

    def step(table, accum, lookup_slots, lookup_weights, touched_rows, pooled_grad):
        small = fits_small(mesh, table, lookup_slots, touched_rows, pooled_grad)
        return jax.shard_map(
            per_device_small if small else per_device_general,
            mesh=mesh,
            in_specs=placed,
            out_specs=(P(("replica", "mp"), None), P("mp", None), P("mp", None)),
            check_vma=False,
        )(table, accum, lookup_slots, lookup_weights, touched_rows, pooled_grad)

    return step
```

```python
import functools
import math

import jax
import jax.numpy as jnp
from jax import lax
from jax.experimental import pallas as pl
from jax.experimental.pallas import tpu as pltpu
from jax.sharding import PartitionSpec as P

learn_rate = 0.5
LANES = 128
MIB = 1 << 20


def build_counts(slots, weights, touch_count):
    bag_count = slots.shape[0]
    block_rows = math.gcd(bag_count, 512)
    columns = jnp.arange(touch_count, dtype=jnp.int32)

    def one_block(block_index):
        slot_block = lax.dynamic_slice_in_dim(slots, block_index * block_rows, block_rows, 0)
        weight_block = lax.dynamic_slice_in_dim(weights, block_index * block_rows, block_rows, 0)
        matches = (slot_block[:, :, None] == columns[None, None, :]).astype(jnp.float32)
        return jnp.sum(matches * weight_block[:, :, None].astype(jnp.float32), axis=1).astype(
            jnp.bfloat16
        )

    blocks = lax.map(one_block, jnp.arange(bag_count // block_rows, dtype=jnp.int32))
    return blocks.reshape(bag_count, touch_count)


def adagrad(row_values, history, gradient):
    history_new = history + gradient * gradient
    return (row_values - learn_rate * gradient / jnp.sqrt(history_new), history_new)


def per_device_general(table, accum, lookup_slots, lookup_weights, touched_rows, pooled_grad):
    touch_count = touched_rows.shape[0]
    feature_dim = table.shape[1]
    bag_local = pooled_grad.shape[0]
    mp_count = lax.axis_size("mp")
    counts = build_counts(lookup_slots, lookup_weights, touch_count)
    row_tile = table[touched_rows]
    tile_low = row_tile.astype(jnp.bfloat16)
    partial_value = jnp.dot(counts, tile_low, preferred_element_type=jnp.float32)
    received = lax.all_to_all(
        partial_value.reshape(mp_count, bag_local, feature_dim),
        "mp",
        split_axis=0,
        concat_axis=0,
        tiled=True,
    )
    pooled = jnp.sum(received, axis=0)
    local_grad = lax.dot_general(
        counts,
        lax.all_gather(pooled_grad, "mp", axis=0, tiled=True),
        (((0,), (0,)), ((), ())),
        preferred_element_type=jnp.float32,
    )
    gradient = lax.psum(local_grad.astype(jnp.bfloat16), "replica").astype(jnp.float32)
    new_rows, new_history = adagrad(row_tile, accum[touched_rows], gradient)
    new_table = table.at[touched_rows].set(new_rows)
    new_accum = accum.at[touched_rows].set(new_history)
    return (pooled, new_table, new_accum)


def vmem():
    return pl.BlockSpec(memory_space=pltpu.VMEM)


def smem():
    return pl.BlockSpec(memory_space=pltpu.SMEM)


def hbm():
    return pl.BlockSpec(memory_space=pltpu.HBM)


def in_hbm(value):
    return pltpu.with_memory_space_constraint(value, pltpu.HBM)


def params(mib):
    return pltpu.CompilerParams(vmem_limit_bytes=mib * MIB)


def pack_kernel(grad_hbm, slots_hbm, weights_hbm, out_ref, slots_ref, weights_ref, slot_rows, weight_rows, sem):
    hots, bags = slots_ref.shape
    rows = grad_hbm.shape[0]
    blocks = bags // LANES
    loads = [
        pltpu.make_async_copy(slots_hbm, slots_ref, sem.at[0]),
        pltpu.make_async_copy(weights_hbm, weights_ref, sem.at[1]),
        pltpu.make_async_copy(grad_hbm, out_ref.at[pl.ds(0, rows), :], sem.at[2]),
    ]
    for load in loads:
        load.start()
    for load in loads:
        load.wait()
    for h in range(hots):
        for j in range(blocks):
            slot_rows[pl.ds(h * blocks + j, 1), :] = slots_ref[pl.ds(h, 1), pl.ds(j * LANES, LANES)]
            weight_rows[pl.ds(h * blocks + j, 1), :] = weights_ref[pl.ds(h, 1), pl.ds(j * LANES, LANES)]
    slot = slot_rows[...]
    code = weight_rows[...] * 64 + lax.shift_right_logical(slot, 8)
    low = jnp.bitwise_and(slot, 255)
    lookups = hots * blocks
    out_ref[pl.ds(rows, lookups), :] = low.astype(jnp.float32).astype(jnp.bfloat16)
    out_ref[pl.ds(rows + lookups, lookups), :] = code.astype(jnp.float32).astype(jnp.bfloat16)


def fill_counts(packed_ref, counts_ref, first, me, mp, hots, low_rows, code_rows):
    touch = counts_ref.shape[0]
    lookups = low_rows.shape[0]
    rows = packed_ref.shape[0] - 2 * lookups
    blocks = lookups // hots
    low_rows[...] = packed_ref[pl.ds(rows, lookups), :].astype(jnp.float32)
    code_rows[...] = packed_ref[pl.ds(rows + lookups, lookups), :].astype(jnp.float32)
    step = min(touch, 256)
    line = lax.broadcasted_iota(jnp.int32, (step, LANES), 0).astype(jnp.float32).astype(jnp.bfloat16)
    zero = jnp.zeros((step, LANES), jnp.bfloat16)

    def one(j, carry):
        distance = jnp.bitwise_xor(j * LANES // rows, me)
        half = jnp.bitwise_and(distance, 1) * (blocks * LANES // 2)
        at_column = half + lax.shift_right_logical(distance, 1) * rows + j * LANES % rows + first
        columns = pl.ds(pl.multiple_of(at_column, LANES), LANES)
        lows, highs, weights = [], [], []
        for h in range(hots):
            low = low_rows[pl.ds(h * blocks + j, 1), :]
            code = code_rows[pl.ds(h * blocks + j, 1), :].astype(jnp.int32)
            lows.append(low)
            highs.append(jnp.bitwise_and(code, 63))
            weights.append(lax.shift_right_logical(code, 6).astype(jnp.float32).astype(jnp.bfloat16))
        for k in range(touch // step):
            total = None
            for h in range(hots):
                at = jnp.where(highs[h] == k, lows[h], -1.0).astype(jnp.bfloat16)
                at = jnp.broadcast_to(at, (step, LANES))
                term = jnp.where(at == line, jnp.broadcast_to(weights[h], (step, LANES)), zero)
                total = term if total is None else total + term
            counts_ref[pl.ds(k * step, step), columns] = total
        return carry

    lax.fori_loop(0, blocks, one, 0)


def pooled_kernel(hots, mp, touched_hbm, packed_ref, peer_ref, table_hbm, keep_ref, send_ref, counts_ref,
                  table_vmem, tile, low_rows, code_rows, sum_t, touched_ref, sem):
    touch = touched_ref.shape[0]
    bags = counts_ref.shape[1] // 2
    rows = bags // mp
    blocks = bags // LANES
    me = lax.axis_index("mp")
    loads = [
        pltpu.make_async_copy(touched_hbm, touched_ref, sem.at[0]),
        pltpu.make_async_copy(table_hbm, table_vmem, sem.at[1]),
    ]
    for load in loads:
        load.start()

    for d, ref in enumerate((packed_ref, peer_ref)):
        fill_counts(ref, counts_ref, d * bags, me, mp, hots, low_rows, code_rows)
    for load in loads:
        load.wait()

    def gather(i, carry):
        for u in range(16):
            t = i * 16 + u
            tile[pl.ds(t, 1), :] = table_vmem[pl.ds(touched_ref[t], 1), :]
        return carry

    lax.fori_loop(0, touch // 16, gather, 0)
    tile_t = tile[...].T.astype(jnp.bfloat16)
    sum_t[...] = jnp.dot(tile_t, counts_ref[:, pl.ds(0, bags)], preferred_element_type=jnp.float32)
    for half, ref in ((0, keep_ref), (bags // 2, send_ref)):
        for c in range(mp // 2):
            ref[c] = sum_t[:, pl.ds(half + c * rows, rows)].T


def join_kernel(rows, replicas, keep_ref, send_ref, *refs):
    packed, outs = refs[:replicas], refs[replicas:]
    for c, out_ref in enumerate(outs):
        for d, ref in enumerate(packed):
            out_ref[pl.ds(d * rows, rows), :] = ref[pl.ds(0, rows), :]
        out_ref[pl.ds(replicas * rows, rows), :] = keep_ref[c].astype(jnp.bfloat16)
        out_ref[pl.ds((replicas + 1) * rows, rows), :] = send_ref[c].astype(jnp.bfloat16)


def counts_kernel(hots, mp, touched_hbm, touched_rows_ref, accum_hbm, *refs):
    peers, refs = refs[:-8], refs[-8:]
    counts_ref, accum_ref, history_ref, spread_ref, low_rows, code_rows, touched_ref, sem = refs
    loads = [
        pltpu.make_async_copy(touched_hbm, touched_ref, sem.at[0]),
        pltpu.make_async_copy(accum_hbm, accum_ref, sem.at[1]),
    ]
    for load in loads:
        load.start()
    bags = counts_ref.shape[1] // len(peers)
    me = lax.axis_index("mp")
    for d, ref in enumerate(peers):
        fill_counts(ref, counts_ref, d * bags, me, mp, hots, low_rows, code_rows)

    step = 256
    line = lax.broadcasted_iota(jnp.int32, (step, LANES), 0).astype(jnp.float32).astype(jnp.bfloat16)
    one, zero = jnp.ones((step, LANES), jnp.bfloat16), jnp.zeros((step, LANES), jnp.bfloat16)

    def spread(j, carry):
        row = touched_rows_ref[pl.ds(j, 1), :]
        high = lax.shift_right_logical(row, 8)
        low = jnp.bitwise_and(row, 255).astype(jnp.float32)
        columns = pl.ds(pl.multiple_of(j * LANES, LANES), LANES)
        for k in range(spread_ref.shape[0] // step):
            at = jnp.where(high == k, low, -1.0).astype(jnp.bfloat16)
            spread_ref[pl.ds(k * step, step), columns] = jnp.where(
                jnp.broadcast_to(at, (step, LANES)) == line, one, zero
            )
        return carry

    lax.fori_loop(0, spread_ref.shape[1] // LANES, spread, 0)
    for load in loads:
        load.wait()

    def gather(i, carry):
        for u in range(16):
            t = i * 16 + u
            history_ref[pl.ds(t, 1), :] = accum_ref[pl.ds(touched_ref[t], 1), :]
        return carry

    lax.fori_loop(0, history_ref.shape[0] // 16, gather, 0)


def hold_kernel(*refs):
    del refs


def hold(values, others):
    n = len(values)
    return pl.pallas_call(
        hold_kernel,
        out_shape=[jax.ShapeDtypeStruct(v.shape, v.dtype) for v in values],
        in_specs=[pl.BlockSpec(memory_space=pl.ANY)] * (n + len(others)),
        out_specs=[pl.BlockSpec(memory_space=pl.ANY)] * n,
        input_output_aliases={i: i for i in range(n)},
        compiler_params=params(1),
        name="hold",
    )(*values, *others)


def parity_sum(odd, rows, replicas, near_ref, rest_ref, blocks, grads):
    span = len(blocks) * rows
    for c, ref in enumerate(blocks):
        for d in range(replicas):
            grads[pl.ds(d * span + c * rows, rows), :] = ref[pl.ds(d * rows, rows), :]
    total = None
    for d in range(replicas):
        held, place = (near_ref, d) if d < replicas // 2 else (rest_ref, d - replicas // 2)
        columns = pl.ds((2 * place + odd) * span, span)
        term = jnp.dot(held[:, columns], grads[pl.ds(d * span, span), :], preferred_element_type=jnp.float32)
        total = term if total is None else total + term
    return total


def grad_kernel(rows, replicas, near_ref, rest_ref, *refs):
    blocks, sum_ref, grads = refs[:-2], refs[-2], refs[-1]
    sum_ref[...] = parity_sum(0, rows, replicas, near_ref, rest_ref, blocks, grads)


def update_kernel(parts, rows, replicas, near_ref, rest_ref, first_ref, history_ref, spread_ref, table_ref, accum_ref,
                  keep_ref, *refs):
    far, blocks, refs = refs[:parts - 1], refs[parts - 1:2 * parts - 1], refs[2 * parts - 1:]
    new_table_ref, new_accum_ref, pooled_ref, grads, change, table_vmem, accum_vmem, out_sem = refs
    width = first_ref.shape[1]
    gradient = first_ref[...] + parity_sum(1, rows, replicas, near_ref, rest_ref, blocks, grads)
    square = gradient * gradient
    step = learn_rate * gradient * lax.rsqrt(history_ref[...] + square)
    change[:, pl.ds(0, width)] = step.astype(jnp.bfloat16)
    change[:, pl.ds(width, width)] = square.astype(jnp.bfloat16)
    chunks = 8
    size = table_vmem.shape[0] // chunks
    stores = []
    for c in range(chunks):
        part = pl.ds(c * size, size)
        full = jnp.dot(spread_ref[part, :], change[...], preferred_element_type=jnp.float32)
        table_vmem[part, :] = table_ref[part, :] - full[:, :width]
        accum_vmem[part, :] = accum_ref[part, :] + full[:, width:]
        for held, out, s in ((table_vmem, new_table_ref, 0), (accum_vmem, new_accum_ref, 1)):
            store = pltpu.make_async_copy(held.at[part, :], out.at[part, :], out_sem.at[s, c])
            store.start()
            stores.append(store)
    pooled = keep_ref[0]
    for ref in far:
        pooled = pooled + ref[pl.ds(replicas * rows, rows), :].astype(jnp.float32)
    for ref in blocks:
        pooled = pooled + ref[pl.ds((replicas + 1) * rows, rows), :].astype(jnp.float32)
    pooled_ref[...] = pooled
    for store in stores:
        store.wait()


def per_device_small(table, accum, lookup_slots, lookup_weights, touched_rows, pooled_grad):
    bags, hots = lookup_slots.shape
    touch = touched_rows.shape[0]
    rows, feature = pooled_grad.shape
    table_rows = table.shape[0]
    mp = lax.axis_size("mp")
    replicas = lax.axis_size("replica")
    lookups = hots * (bags // LANES)
    low = jnp.bfloat16

    def swap(value, axis, distance):
        return lax.ppermute(value, axis, [(i, i ^ distance) for i in range(lax.axis_size(axis))])

    packed = pl.pallas_call(
        pack_kernel,
        out_shape=jax.ShapeDtypeStruct((rows + 2 * lookups, LANES), low),
        in_specs=[hbm()] * 3,
        out_specs=vmem(),
        scratch_shapes=[pltpu.VMEM((hots, bags), jnp.int32)] * 2
        + [pltpu.VMEM((lookups, LANES), jnp.int32)] * 2
        + [pltpu.SemaphoreType.DMA((3,))],
        compiler_params=params(8),
        name="pack",
    )(in_hbm(pooled_grad), in_hbm(lookup_slots.T), in_hbm(lookup_weights.T))
    peers = [swap(packed, "replica", d) for d in range(1, replicas)]

    keep, send, near_counts, table_held = pl.pallas_call(
        functools.partial(pooled_kernel, hots, mp),
        out_shape=[
            jax.ShapeDtypeStruct((mp // 2, rows, feature), jnp.float32),
            jax.ShapeDtypeStruct((mp // 2, rows, feature), jnp.float32),
            jax.ShapeDtypeStruct((touch, 2 * bags), low),
            jax.ShapeDtypeStruct((table_rows, feature), jnp.float32),
        ],
        in_specs=[hbm(), vmem(), vmem(), hbm()],
        out_specs=[vmem()] * 4,
        scratch_shapes=[
            pltpu.VMEM((touch, feature), jnp.float32),
            pltpu.VMEM((lookups, LANES), jnp.float32),
            pltpu.VMEM((lookups, LANES), jnp.float32),
            pltpu.VMEM((feature, bags), jnp.float32),
            pltpu.SMEM((touch,), jnp.int32),
            pltpu.SemaphoreType.DMA((2,)),
        ],
        compiler_params=params(20),
        cost_estimate=pl.CostEstimate(flops=2 * touch * bags * feature, bytes_accessed=8 * MIB, transcendentals=0),
        name="pool",
    )(in_hbm(touched_rows), packed, peers[0], in_hbm(table))

    parts = mp // 2
    payloads = pl.pallas_call(
        functools.partial(join_kernel, rows, replicas),
        out_shape=[jax.ShapeDtypeStruct(((replicas + 2) * rows, feature), low)] * parts,
        in_specs=[vmem()] * (2 + replicas),
        out_specs=[vmem()] * parts,
        compiler_params=params(8),
        name="join",
    )(keep, send, packed, *peers)
    far = [swap(payloads[c], "mp", 2 * c) for c in range(1, parts)]

    rest_counts, accum_held, history, spread = pl.pallas_call(
        functools.partial(counts_kernel, hots, mp),
        out_shape=[
            jax.ShapeDtypeStruct((touch, bags * (replicas - 2)), low),
            jax.ShapeDtypeStruct((table_rows, feature), jnp.float32),
            jax.ShapeDtypeStruct((touch, feature), jnp.float32),
            jax.ShapeDtypeStruct((table_rows, touch), low),
        ],
        in_specs=[hbm(), vmem(), hbm()] + [vmem()] * (replicas - 2),
        out_specs=[vmem()] * 4,
        scratch_shapes=[pltpu.VMEM((lookups, LANES), jnp.float32)] * 2
        + [pltpu.SMEM((touch,), jnp.int32), pltpu.SemaphoreType.DMA((2,))],
        compiler_params=params(24),
        cost_estimate=pl.CostEstimate(flops=0, bytes_accessed=1024, transcendentals=0),
        name="count",
    )(in_hbm(touched_rows), touched_rows.reshape(touch // LANES, LANES), in_hbm(accum), *peers[1:])

    same = [payloads[0], *hold(far, [rest_counts])]
    other = [swap(value, "mp", 1) for value in same]

    first = pl.pallas_call(
        functools.partial(grad_kernel, rows, replicas),
        out_shape=jax.ShapeDtypeStruct((touch, feature), jnp.float32),
        in_specs=[vmem()] * (2 + mp // 2),
        out_specs=vmem(),
        scratch_shapes=[pltpu.VMEM((bags * replicas // 2, feature), low)],
        compiler_params=params(16),
        cost_estimate=pl.CostEstimate(flops=0, bytes_accessed=1024, transcendentals=0),
        name="gradient",
    )(near_counts, rest_counts, *same)

    new_table, new_accum, pooled = pl.pallas_call(
        functools.partial(update_kernel, parts, rows, replicas),
        out_shape=[jax.ShapeDtypeStruct(table.shape, jnp.float32)] * 2
        + [jax.ShapeDtypeStruct((rows, feature), jnp.float32)],
        in_specs=[vmem()] * (7 + 2 * parts),
        out_specs=[hbm()] * 2 + [vmem()],
        scratch_shapes=[
            pltpu.VMEM((bags * replicas // 2, feature), low),
            pltpu.VMEM((touch, 2 * feature), low),
            pltpu.VMEM((table_rows, feature), jnp.float32),
            pltpu.VMEM((table_rows, feature), jnp.float32),
            pltpu.SemaphoreType.DMA((2, 8)),
        ],
        compiler_params=params(24),
        cost_estimate=pl.CostEstimate(flops=0, bytes_accessed=MIB, transcendentals=0),
        name="update",
    )(near_counts, rest_counts, first, history, spread, table_held, accum_held, keep, *same[1:], *other)
    return (pooled, new_table, new_accum)


def fits_small(mesh, table, lookup_slots, touched_rows, pooled_grad):
    mp, replicas = mesh.shape["mp"], mesh.shape["replica"]
    powers = all(n & (n - 1) == 0 for n in (mp, replicas))
    touch = touched_rows.shape[0] // mp
    bags = lookup_slots.shape[0] // replicas
    rows = pooled_grad.shape[0] // (mp * replicas)
    return (
        powers
        and 2 <= mp <= 8
        and replicas == 4
        and lookup_slots.shape[0] * touch <= 4096 * 1024
        and touch % 256 == 0
        and touch <= 16384
        and bags % LANES == 0
        and rows % LANES == 0
        and table.shape[1] == LANES
        and table.shape[0] // mp <= 4096
        and table.shape[0] // mp % 256 == 0
        and touch % LANES == 0
    )


def solution(mesh):
    placed = (
        P("mp", None),
        P("mp", None),
        P("replica", "mp"),
        P("replica", "mp"),
        P("mp"),
        P(("replica", "mp"), None),
    )

    def step(table, accum, lookup_slots, lookup_weights, touched_rows, pooled_grad):
        small = fits_small(mesh, table, lookup_slots, touched_rows, pooled_grad)
        return jax.shard_map(
            per_device_small if small else per_device_general,
            mesh=mesh,
            in_specs=placed,
            out_specs=(P(("replica", "mp"), None), P("mp", None), P("mp", None)),
            check_vma=False,
        )(table, accum, lookup_slots, lookup_weights, touched_rows, pooled_grad)

    return step
```

```python
import functools
import math

import jax
import jax.numpy as jnp
from jax import lax
from jax.experimental import pallas as pl
from jax.experimental.pallas import tpu as pltpu
from jax.sharding import PartitionSpec as P

learn_rate = 0.5
LANES = 128
MIB = 1 << 20


def build_counts(slots, weights, touch_count):
    bag_count = slots.shape[0]
    block_rows = math.gcd(bag_count, 512)
    columns = jnp.arange(touch_count, dtype=jnp.int32)

    def one_block(block_index):
        slot_block = lax.dynamic_slice_in_dim(slots, block_index * block_rows, block_rows, 0)
        weight_block = lax.dynamic_slice_in_dim(weights, block_index * block_rows, block_rows, 0)
        matches = (slot_block[:, :, None] == columns[None, None, :]).astype(jnp.float32)
        return jnp.sum(matches * weight_block[:, :, None].astype(jnp.float32), axis=1).astype(
            jnp.bfloat16
        )

    blocks = lax.map(one_block, jnp.arange(bag_count // block_rows, dtype=jnp.int32))
    return blocks.reshape(bag_count, touch_count)


def adagrad(row_values, history, gradient):
    history_new = history + gradient * gradient
    return (row_values - learn_rate * gradient / jnp.sqrt(history_new), history_new)


def per_device_general(table, accum, lookup_slots, lookup_weights, touched_rows, pooled_grad):
    touch_count = touched_rows.shape[0]
    feature_dim = table.shape[1]
    bag_local = pooled_grad.shape[0]
    mp_count = lax.axis_size("mp")
    counts = build_counts(lookup_slots, lookup_weights, touch_count)
    row_tile = table[touched_rows]
    tile_low = row_tile.astype(jnp.bfloat16)
    partial_value = jnp.dot(counts, tile_low, preferred_element_type=jnp.float32)
    received = lax.all_to_all(
        partial_value.reshape(mp_count, bag_local, feature_dim),
        "mp",
        split_axis=0,
        concat_axis=0,
        tiled=True,
    )
    pooled = jnp.sum(received, axis=0)
    local_grad = lax.dot_general(
        counts,
        lax.all_gather(pooled_grad, "mp", axis=0, tiled=True),
        (((0,), (0,)), ((), ())),
        preferred_element_type=jnp.float32,
    )
    gradient = lax.psum(local_grad.astype(jnp.bfloat16), "replica").astype(jnp.float32)
    new_rows, new_history = adagrad(row_tile, accum[touched_rows], gradient)
    new_table = table.at[touched_rows].set(new_rows)
    new_accum = accum.at[touched_rows].set(new_history)
    return (pooled, new_table, new_accum)


def vmem():
    return pl.BlockSpec(memory_space=pltpu.VMEM)


def smem():
    return pl.BlockSpec(memory_space=pltpu.SMEM)


def hbm():
    return pl.BlockSpec(memory_space=pltpu.HBM)


def in_hbm(value):
    return pltpu.with_memory_space_constraint(value, pltpu.HBM)


def params(mib):
    return pltpu.CompilerParams(vmem_limit_bytes=mib * MIB)


def pack_kernel(grad_hbm, slots_hbm, weights_hbm, out_ref, slots_ref, weights_ref, slot_rows, weight_rows, sem):
    hots, bags = slots_ref.shape
    rows = grad_hbm.shape[0]
    blocks = bags // LANES
    loads = [
        pltpu.make_async_copy(slots_hbm, slots_ref, sem.at[0]),
        pltpu.make_async_copy(weights_hbm, weights_ref, sem.at[1]),
        pltpu.make_async_copy(grad_hbm, out_ref.at[pl.ds(0, rows), :], sem.at[2]),
    ]
    for load in loads:
        load.start()
    for load in loads:
        load.wait()
    for h in range(hots):
        for j in range(blocks):
            slot_rows[pl.ds(h * blocks + j, 1), :] = slots_ref[pl.ds(h, 1), pl.ds(j * LANES, LANES)]
            weight_rows[pl.ds(h * blocks + j, 1), :] = weights_ref[pl.ds(h, 1), pl.ds(j * LANES, LANES)]
    slot = slot_rows[...]
    code = weight_rows[...] * 64 + lax.shift_right_logical(slot, 8)
    low = jnp.bitwise_and(slot, 255)
    lookups = hots * blocks
    out_ref[pl.ds(rows, lookups), :] = low.astype(jnp.float32).astype(jnp.bfloat16)
    out_ref[pl.ds(rows + lookups, lookups), :] = code.astype(jnp.float32).astype(jnp.bfloat16)


def fill_counts(packed_ref, counts_ref, place, me, hots, low_rows, code_rows):
    touch = counts_ref.shape[0]
    lookups = low_rows.shape[0]
    rows = packed_ref.shape[0] - 2 * lookups
    blocks = lookups // hots
    low_rows[...] = packed_ref[pl.ds(rows, lookups), :].astype(jnp.float32)
    code_rows[...] = packed_ref[pl.ds(rows + lookups, lookups), :].astype(jnp.float32)
    step = min(touch, 256)
    line = lax.broadcasted_iota(jnp.int32, (step, LANES), 0).astype(jnp.float32).astype(jnp.bfloat16)
    zero = jnp.zeros((step, LANES), jnp.bfloat16)

    def one(j, carry):
        distance = jnp.bitwise_xor(j * LANES // rows, me)
        half = jnp.bitwise_and(distance, 1) * (counts_ref.shape[1] // 2) + place * (blocks * LANES // 2)
        at_column = half + lax.shift_right_logical(distance, 1) * rows + j * LANES % rows
        columns = pl.ds(pl.multiple_of(at_column, LANES), LANES)
        lows, highs, weights = [], [], []
        for h in range(hots):
            low = low_rows[pl.ds(h * blocks + j, 1), :]
            code = code_rows[pl.ds(h * blocks + j, 1), :].astype(jnp.int32)
            lows.append(low)
            highs.append(jnp.bitwise_and(code, 63))
            weights.append(lax.shift_right_logical(code, 6).astype(jnp.float32).astype(jnp.bfloat16))
        for k in range(touch // step):
            total = None
            for h in range(hots):
                at = jnp.where(highs[h] == k, lows[h], -1.0).astype(jnp.bfloat16)
                at = jnp.broadcast_to(at, (step, LANES))
                term = jnp.where(at == line, jnp.broadcast_to(weights[h], (step, LANES)), zero)
                total = term if total is None else total + term
            counts_ref[pl.ds(k * step, step), columns] = total
        return carry

    lax.fori_loop(0, blocks, one, 0)


def pooled_kernel(hots, mp, touched_hbm, packed_ref, table_hbm, keep_ref, send_ref, counts_ref,
                  table_vmem, tile, low_rows, code_rows, sum_t, touched_ref, sem):
    touch = touched_ref.shape[0]
    bags = counts_ref.shape[1]
    rows = bags // mp
    blocks = bags // LANES
    me = lax.axis_index("mp")
    loads = [
        pltpu.make_async_copy(touched_hbm, touched_ref, sem.at[0]),
        pltpu.make_async_copy(table_hbm, table_vmem, sem.at[1]),
    ]
    for load in loads:
        load.start()

    fill_counts(packed_ref, counts_ref, 0, me, hots, low_rows, code_rows)
    for load in loads:
        load.wait()

    def gather(i, carry):
        for u in range(16):
            t = i * 16 + u
            tile[pl.ds(t, 1), :] = table_vmem[pl.ds(touched_ref[t], 1), :]
        return carry

    lax.fori_loop(0, touch // 16, gather, 0)
    tile_t = tile[...].T.astype(jnp.bfloat16)
    for half in (0, 1):
        sum_t[:, pl.ds(half * (bags // 2), bags // 2)] = jnp.dot(
            tile_t, counts_ref[:, pl.ds(half * (bags // 2), bags // 2)], preferred_element_type=jnp.float32
        )
    for half, ref in ((0, keep_ref), (bags // 2, send_ref)):
        for c in range(mp // 2):
            ref[c] = sum_t[:, pl.ds(half + c * rows, rows)].T


def join_kernel(rows, replicas, keep_ref, send_ref, *refs):
    packed, outs = refs[:replicas], refs[replicas:]
    for c, out_ref in enumerate(outs):
        for d, ref in enumerate(packed):
            out_ref[pl.ds(d * rows, rows), :] = ref[pl.ds(0, rows), :]
        out_ref[pl.ds(replicas * rows, rows), :] = send_ref[c].astype(jnp.bfloat16)
        out_ref[pl.ds((replicas + 1) * rows, rows), :] = keep_ref[c].astype(jnp.bfloat16)


def counts_kernel(hots, touched_hbm, touched_rows_ref, accum_hbm, *refs):
    peers, refs = refs[:-8], refs[-8:]
    counts_ref, accum_ref, history_ref, spread_ref, low_rows, code_rows, touched_ref, sem = refs
    loads = [
        pltpu.make_async_copy(touched_hbm, touched_ref, sem.at[0]),
        pltpu.make_async_copy(accum_hbm, accum_ref, sem.at[1]),
    ]
    for load in loads:
        load.start()
    me = lax.axis_index("mp")
    for d, ref in enumerate(peers):
        fill_counts(ref, counts_ref, d, me, hots, low_rows, code_rows)

    step = 256
    line = lax.broadcasted_iota(jnp.int32, (step, LANES), 0).astype(jnp.float32).astype(jnp.bfloat16)
    one, zero = jnp.ones((step, LANES), jnp.bfloat16), jnp.zeros((step, LANES), jnp.bfloat16)

    def spread(j, carry):
        row = touched_rows_ref[pl.ds(j, 1), :]
        high = lax.shift_right_logical(row, 8)
        low = jnp.bitwise_and(row, 255).astype(jnp.float32)
        columns = pl.ds(pl.multiple_of(j * LANES, LANES), LANES)
        for k in range(spread_ref.shape[0] // step):
            at = jnp.where(high == k, low, -1.0).astype(jnp.bfloat16)
            spread_ref[pl.ds(k * step, step), columns] = jnp.where(
                jnp.broadcast_to(at, (step, LANES)) == line, one, zero
            )
        return carry

    lax.fori_loop(0, spread_ref.shape[1] // LANES, spread, 0)
    for load in loads:
        load.wait()

    def gather(i, carry):
        for u in range(16):
            t = i * 16 + u
            history_ref[pl.ds(t, 1), :] = accum_ref[pl.ds(touched_ref[t], 1), :]
        return carry

    lax.fori_loop(0, history_ref.shape[0] // 16, gather, 0)


def merge_kernel(rows, keep_ref, waited_ref, *refs):
    del waited_ref
    blocks, merged_ref, pooled_ref = refs[:-2], refs[-2], refs[-1]
    span = merged_ref.shape[0] // len(blocks)
    total = keep_ref[0]
    for c, ref in enumerate(blocks):
        merged_ref[pl.ds(c * span, span), :] = ref[pl.ds(0, span), :]
        if c:
            total = total + ref[pl.ds(span, rows), :].astype(jnp.float32)
    pooled_ref[...] = total


def parity_sum(odd, parts, rows, near_ref, rest_ref, blocks, grads):
    span = parts * rows
    replicas = grads.shape[0] // span
    for c in range(parts):
        for d in range(replicas):
            grads[pl.ds(d * span + c * rows, rows), :] = blocks[pl.ds((c * (replicas + 1) + d) * rows, rows), :]
    near = near_ref.shape[1] // 2
    rest = rest_ref.shape[1] // 2
    return jnp.dot(
        near_ref[:, pl.ds(odd * near, near)], grads[pl.ds(0, near), :], preferred_element_type=jnp.float32
    ) + jnp.dot(
        rest_ref[:, pl.ds(odd * rest, rest)], grads[pl.ds(near, rest), :], preferred_element_type=jnp.float32
    )


def grad_kernel(parts, rows, near_ref, rest_ref, blocks, sum_ref, grads):
    sum_ref[...] = parity_sum(0, parts, rows, near_ref, rest_ref, blocks, grads)


def update_kernel(parts, rows, near_ref, rest_ref, first_ref, history_ref, spread_ref, table_ref, accum_ref,
                  sum_ref, blocks, new_table_ref, new_accum_ref, pooled_ref, grads, change, table_vmem, accum_vmem,
                  pooled_vmem, out_sem):
    width = first_ref.shape[1]
    chunks = 8
    pooled = sum_ref[...]
    span = blocks.shape[0] // parts
    for c in range(parts):
        pooled = pooled + blocks[pl.ds((c + 1) * span - rows, rows), :].astype(jnp.float32)
    pooled_vmem[...] = pooled
    stores = [pltpu.make_async_copy(pooled_vmem, pooled_ref, out_sem.at[2, 0])]
    stores[0].start()
    gradient = first_ref[...] + parity_sum(1, parts, rows, near_ref, rest_ref, blocks, grads)
    square = gradient * gradient
    step = learn_rate * gradient * lax.rsqrt(history_ref[...] + square)
    change[:, pl.ds(0, width)] = step.astype(jnp.bfloat16)
    change[:, pl.ds(width, width)] = square.astype(jnp.bfloat16)
    size = table_vmem.shape[0] // chunks

    def spread(c):
        return jnp.dot(spread_ref[pl.ds(c * size, size), :], change[...], preferred_element_type=jnp.float32)

    ahead = spread(0)
    for c in range(chunks):
        part = pl.ds(c * size, size)
        full = ahead
        if c + 1 < chunks:
            ahead = spread(c + 1)
        table_vmem[part, :] = table_ref[part, :] - full[:, :width]
        accum_vmem[part, :] = accum_ref[part, :] + full[:, width:]
        for held, out, s in ((table_vmem, new_table_ref, 0), (accum_vmem, new_accum_ref, 1)):
            store = pltpu.make_async_copy(held.at[part, :], out.at[part, :], out_sem.at[s, c])
            store.start()
            stores.append(store)
    for store in stores:
        store.wait()


def per_device_small(table, accum, lookup_slots, lookup_weights, touched_rows, pooled_grad):
    bags, hots = lookup_slots.shape
    touch = touched_rows.shape[0]
    rows, feature = pooled_grad.shape
    table_rows = table.shape[0]
    mp = lax.axis_size("mp")
    replicas = lax.axis_size("replica")
    lookups = hots * (bags // LANES)
    low = jnp.bfloat16

    def swap(value, axis, distance):
        return lax.ppermute(value, axis, [(i, i ^ distance) for i in range(lax.axis_size(axis))])

    packed = pl.pallas_call(
        pack_kernel,
        out_shape=jax.ShapeDtypeStruct((rows + 2 * lookups, LANES), low),
        in_specs=[hbm()] * 3,
        out_specs=vmem(),
        scratch_shapes=[pltpu.VMEM((hots, bags), jnp.int32)] * 2
        + [pltpu.VMEM((lookups, LANES), jnp.int32)] * 2
        + [pltpu.SemaphoreType.DMA((3,))],
        compiler_params=params(8),
        name="pack",
    )(in_hbm(pooled_grad), in_hbm(lookup_slots.T), in_hbm(lookup_weights.T))
    peers = [swap(packed, "replica", d) for d in range(1, replicas)]

    keep, send, near_counts, table_held = pl.pallas_call(
        functools.partial(pooled_kernel, hots, mp),
        out_shape=[
            jax.ShapeDtypeStruct((mp // 2, rows, feature), jnp.float32),
            jax.ShapeDtypeStruct((mp // 2, rows, feature), jnp.float32),
            jax.ShapeDtypeStruct((touch, bags), low),
            jax.ShapeDtypeStruct((table_rows, feature), jnp.float32),
        ],
        in_specs=[hbm(), vmem(), hbm()],
        out_specs=[vmem()] * 4,
        scratch_shapes=[
            pltpu.VMEM((touch, feature), jnp.float32),
            pltpu.VMEM((lookups, LANES), jnp.float32),
            pltpu.VMEM((lookups, LANES), jnp.float32),
            pltpu.VMEM((feature, bags), jnp.float32),
            pltpu.SMEM((touch,), jnp.int32),
            pltpu.SemaphoreType.DMA((2,)),
        ],
        compiler_params=params(20),
        cost_estimate=pl.CostEstimate(flops=2 * touch * bags * feature, bytes_accessed=8 * MIB, transcendentals=0),
        name="pool",
    )(in_hbm(touched_rows), packed, in_hbm(table))

    parts = mp // 2
    payloads = pl.pallas_call(
        functools.partial(join_kernel, rows, replicas),
        out_shape=[jax.ShapeDtypeStruct(((replicas + 2) * rows, feature), low)] * parts,
        in_specs=[vmem()] * (2 + replicas),
        out_specs=[vmem()] * parts,
        compiler_params=params(8),
        name="join",
    )(keep, send, packed, *peers)
    far = [swap(payloads[c], "mp", 2 * c) for c in range(1, parts)]

    rest_counts, accum_held, history, spread = pl.pallas_call(
        functools.partial(counts_kernel, hots),
        out_shape=[
            jax.ShapeDtypeStruct((touch, bags * (replicas - 1)), low),
            jax.ShapeDtypeStruct((table_rows, feature), jnp.float32),
            jax.ShapeDtypeStruct((touch, feature), jnp.float32),
            jax.ShapeDtypeStruct((table_rows, touch), low),
        ],
        in_specs=[hbm(), vmem(), hbm()] + [vmem()] * (replicas - 1),
        out_specs=[vmem()] * 4,
        scratch_shapes=[pltpu.VMEM((lookups, LANES), jnp.float32)] * 2
        + [pltpu.SMEM((touch,), jnp.int32), pltpu.SemaphoreType.DMA((2,))],
        compiler_params=params(24),
        cost_estimate=pl.CostEstimate(flops=0, bytes_accessed=1024, transcendentals=0),
        name="count",
    )(in_hbm(touched_rows), touched_rows.reshape(touch // LANES, LANES), in_hbm(accum), *peers)

    same, pooled_sum = pl.pallas_call(
        functools.partial(merge_kernel, rows),
        out_shape=[
            jax.ShapeDtypeStruct((parts * (replicas + 1) * rows, feature), low),
            jax.ShapeDtypeStruct((rows, feature), jnp.float32),
        ],
        in_specs=[vmem(), pl.BlockSpec(memory_space=pl.ANY)] + [vmem()] * parts,
        out_specs=[vmem()] * 2,
        compiler_params=params(8),
        name="merge",
    )(keep, rest_counts, payloads[0], *far)
    other = swap(same, "mp", 1)

    first = pl.pallas_call(
        functools.partial(grad_kernel, parts, rows),
        out_shape=jax.ShapeDtypeStruct((touch, feature), jnp.float32),
        in_specs=[vmem()] * 3,
        out_specs=vmem(),
        scratch_shapes=[pltpu.VMEM((bags * replicas // 2, feature), low)],
        compiler_params=params(16),
        cost_estimate=pl.CostEstimate(flops=0, bytes_accessed=1024, transcendentals=0),
        name="gradient",
    )(near_counts, rest_counts, same)

    new_table, new_accum, pooled = pl.pallas_call(
        functools.partial(update_kernel, parts, rows),
        out_shape=[jax.ShapeDtypeStruct(table.shape, jnp.float32)] * 2
        + [jax.ShapeDtypeStruct((rows, feature), jnp.float32)],
        in_specs=[vmem()] * 9,
        out_specs=[hbm()] * 3,
        scratch_shapes=[
            pltpu.VMEM((bags * replicas // 2, feature), low),
            pltpu.VMEM((touch, 2 * feature), low),
            pltpu.VMEM((table_rows, feature), jnp.float32),
            pltpu.VMEM((table_rows, feature), jnp.float32),
            pltpu.VMEM((rows, feature), jnp.float32),
            pltpu.SemaphoreType.DMA((3, 8)),
        ],
        compiler_params=params(24),
        cost_estimate=pl.CostEstimate(flops=0, bytes_accessed=MIB, transcendentals=0),
        name="update",
    )(near_counts, rest_counts, first, history, spread, table_held, accum_held, pooled_sum, other)
    return (pooled, new_table, new_accum)


def fits_small(mesh, table, lookup_slots, touched_rows, pooled_grad):
    mp, replicas = mesh.shape["mp"], mesh.shape["replica"]
    powers = all(n & (n - 1) == 0 for n in (mp, replicas))
    touch = touched_rows.shape[0] // mp
    bags = lookup_slots.shape[0] // replicas
    rows = pooled_grad.shape[0] // (mp * replicas)
    return (
        powers
        and 2 <= mp <= 8
        and replicas == 4
        and lookup_slots.shape[0] * touch <= 4096 * 1024
        and touch % 256 == 0
        and touch <= 16384
        and bags % LANES == 0
        and rows % LANES == 0
        and table.shape[1] == LANES
        and table.shape[0] // mp <= 4096
        and table.shape[0] // mp % 256 == 0
        and touch % LANES == 0
    )


def solution(mesh):
    placed = (
        P("mp", None),
        P("mp", None),
        P("replica", "mp"),
        P("replica", "mp"),
        P("mp"),
        P(("replica", "mp"), None),
    )

    def step(table, accum, lookup_slots, lookup_weights, touched_rows, pooled_grad):
        small = fits_small(mesh, table, lookup_slots, touched_rows, pooled_grad)
        return jax.shard_map(
            per_device_small if small else per_device_general,
            mesh=mesh,
            in_specs=placed,
            out_specs=(P(("replica", "mp"), None), P("mp", None), P("mp", None)),
            check_vma=False,
        )(table, accum, lookup_slots, lookup_weights, touched_rows, pooled_grad)

    return step
```

```python
import functools
import math

import jax
import jax.numpy as jnp
from jax import lax
from jax.experimental import pallas as pl
from jax.experimental.pallas import tpu as pltpu
from jax.sharding import PartitionSpec as P

learn_rate = 0.5
LANES = 128
MIB = 1 << 20


def build_counts(slots, weights, touch_count):
    bag_count = slots.shape[0]
    block_rows = math.gcd(bag_count, 512)
    columns = jnp.arange(touch_count, dtype=jnp.int32)

    def one_block(block_index):
        slot_block = lax.dynamic_slice_in_dim(slots, block_index * block_rows, block_rows, 0)
        weight_block = lax.dynamic_slice_in_dim(weights, block_index * block_rows, block_rows, 0)
        matches = (slot_block[:, :, None] == columns[None, None, :]).astype(jnp.float32)
        return jnp.sum(matches * weight_block[:, :, None].astype(jnp.float32), axis=1).astype(
            jnp.bfloat16
        )

    blocks = lax.map(one_block, jnp.arange(bag_count // block_rows, dtype=jnp.int32))
    return blocks.reshape(bag_count, touch_count)


def adagrad(row_values, history, gradient):
    history_new = history + gradient * gradient
    return (row_values - learn_rate * gradient / jnp.sqrt(history_new), history_new)


def per_device_general(table, accum, lookup_slots, lookup_weights, touched_rows, pooled_grad):
    touch_count = touched_rows.shape[0]
    feature_dim = table.shape[1]
    bag_local = pooled_grad.shape[0]
    mp_count = lax.axis_size("mp")
    counts = build_counts(lookup_slots, lookup_weights, touch_count)
    row_tile = table[touched_rows]
    tile_low = row_tile.astype(jnp.bfloat16)
    partial_value = jnp.dot(counts, tile_low, preferred_element_type=jnp.float32)
    received = lax.all_to_all(
        partial_value.reshape(mp_count, bag_local, feature_dim),
        "mp",
        split_axis=0,
        concat_axis=0,
        tiled=True,
    )
    pooled = jnp.sum(received, axis=0)
    local_grad = lax.dot_general(
        counts,
        lax.all_gather(pooled_grad, "mp", axis=0, tiled=True),
        (((0,), (0,)), ((), ())),
        preferred_element_type=jnp.float32,
    )
    gradient = lax.psum(local_grad.astype(jnp.bfloat16), "replica").astype(jnp.float32)
    new_rows, new_history = adagrad(row_tile, accum[touched_rows], gradient)
    new_table = table.at[touched_rows].set(new_rows)
    new_accum = accum.at[touched_rows].set(new_history)
    return (pooled, new_table, new_accum)


def vmem():
    return pl.BlockSpec(memory_space=pltpu.VMEM)


def smem():
    return pl.BlockSpec(memory_space=pltpu.SMEM)


def hbm():
    return pl.BlockSpec(memory_space=pltpu.HBM)


def in_hbm(value):
    return pltpu.with_memory_space_constraint(value, pltpu.HBM)


def params(mib):
    return pltpu.CompilerParams(vmem_limit_bytes=mib * MIB)


def pack_kernel(grad_hbm, slots_hbm, weights_hbm, out_ref, slots_ref, weights_ref, slot_rows, weight_rows, sem):
    hots, bags = slots_ref.shape
    rows = grad_hbm.shape[0]
    blocks = bags // LANES
    loads = [
        pltpu.make_async_copy(slots_hbm, slots_ref, sem.at[0]),
        pltpu.make_async_copy(weights_hbm, weights_ref, sem.at[1]),
        pltpu.make_async_copy(grad_hbm, out_ref.at[pl.ds(0, rows), :], sem.at[2]),
    ]
    for load in loads:
        load.start()
    for load in loads:
        load.wait()
    for h in range(hots):
        for j in range(blocks):
            slot_rows[pl.ds(h * blocks + j, 1), :] = slots_ref[pl.ds(h, 1), pl.ds(j * LANES, LANES)]
            weight_rows[pl.ds(h * blocks + j, 1), :] = weights_ref[pl.ds(h, 1), pl.ds(j * LANES, LANES)]
    slot = slot_rows[...]
    code = weight_rows[...] * 64 + lax.shift_right_logical(slot, 8)
    low = jnp.bitwise_and(slot, 255)
    lookups = hots * blocks
    out_ref[pl.ds(rows, lookups), :] = low.astype(jnp.float32).astype(jnp.bfloat16)
    out_ref[pl.ds(rows + lookups, lookups), :] = code.astype(jnp.float32).astype(jnp.bfloat16)


def fill_counts(packed_ref, counts_ref, place, me, hots, low_rows, code_rows):
    touch = counts_ref.shape[0]
    lookups = low_rows.shape[0]
    rows = packed_ref.shape[0] - 2 * lookups
    blocks = lookups // hots
    low_rows[...] = packed_ref[pl.ds(rows, lookups), :].astype(jnp.float32)
    code_rows[...] = packed_ref[pl.ds(rows + lookups, lookups), :].astype(jnp.float32)
    step = min(touch, 256)
    line = lax.broadcasted_iota(jnp.int32, (step, LANES), 0).astype(jnp.float32).astype(jnp.bfloat16)
    zero = jnp.zeros((step, LANES), jnp.bfloat16)

    def one(j, carry):
        distance = jnp.bitwise_xor(j * LANES // rows, me)
        half = jnp.bitwise_and(distance, 1) * (counts_ref.shape[1] // 2) + place * (blocks * LANES // 2)
        at_column = half + lax.shift_right_logical(distance, 1) * rows + j * LANES % rows
        columns = pl.ds(pl.multiple_of(at_column, LANES), LANES)
        lows, highs, weights = [], [], []
        for h in range(hots):
            low = low_rows[pl.ds(h * blocks + j, 1), :]
            code = code_rows[pl.ds(h * blocks + j, 1), :].astype(jnp.int32)
            lows.append(low)
            highs.append(jnp.bitwise_and(code, 63))
            weights.append(lax.shift_right_logical(code, 6).astype(jnp.float32).astype(jnp.bfloat16))
        for k in range(touch // step):
            total = None
            for h in range(hots):
                at = jnp.where(highs[h] == k, lows[h], -1.0).astype(jnp.bfloat16)
                at = jnp.broadcast_to(at, (step, LANES))
                term = jnp.where(at == line, jnp.broadcast_to(weights[h], (step, LANES)), zero)
                total = term if total is None else total + term
            counts_ref[pl.ds(k * step, step), columns] = total
        return carry

    lax.fori_loop(0, blocks, one, 0)


def pooled_kernel(hots, mp, touched_hbm, packed_ref, table_hbm, keep_ref, send_ref, counts_ref,
                  table_vmem, tile, low_rows, code_rows, sum_t, touched_ref, sem):
    touch = touched_ref.shape[0]
    bags = counts_ref.shape[1]
    rows = bags // mp
    blocks = bags // LANES
    me = lax.axis_index("mp")
    loads = [
        pltpu.make_async_copy(touched_hbm, touched_ref, sem.at[0]),
        pltpu.make_async_copy(table_hbm, table_vmem, sem.at[1]),
    ]
    for load in loads:
        load.start()

    fill_counts(packed_ref, counts_ref, 0, me, hots, low_rows, code_rows)
    for load in loads:
        load.wait()

    def gather(i, carry):
        for u in range(16):
            t = i * 16 + u
            tile[pl.ds(t, 1), :] = table_vmem[pl.ds(touched_ref[t], 1), :]
        return carry

    lax.fori_loop(0, touch // 16, gather, 0)
    tile_t = tile[...].T.astype(jnp.bfloat16)
    for half in (0, 1):
        sum_t[:, pl.ds(half * (bags // 2), bags // 2)] = jnp.dot(
            tile_t, counts_ref[:, pl.ds(half * (bags // 2), bags // 2)], preferred_element_type=jnp.float32
        )
    for half, ref in ((0, keep_ref), (bags // 2, send_ref)):
        for c in range(mp // 2):
            ref[c] = sum_t[:, pl.ds(half + c * rows, rows)].T


def join_kernel(rows, *refs):
    out_ref = refs[-1]
    for d, ref in enumerate(refs[:-1]):
        out_ref[pl.ds(d * rows, rows), :] = ref[pl.ds(0, rows), :]


def halves_kernel(rows, keep_ref, got_ref, own_ref, next_ref, out_ref):
    own_ref[...] = keep_ref[0] + got_ref[0]
    next_ref[...] = keep_ref[2] + got_ref[2]
    for place, c in ((0, 1), (1, 3)):
        out_ref[pl.ds(place * rows, rows), :] = (keep_ref[c] + got_ref[c]).astype(jnp.bfloat16)


def fold_kernel(rows, own_ref, next_ref, got_ref, own_out, next_out):
    own_out[...] = own_ref[...] + got_ref[pl.ds(0, rows), :].astype(jnp.float32)
    next_out[...] = next_ref[...] + got_ref[pl.ds(rows, rows), :].astype(jnp.float32)


def counts_kernel(hots, accum_hbm, *refs):
    peers, (counts_ref, accum_ref, low_rows, code_rows, sem) = refs[:-5], refs[-5:]
    load = pltpu.make_async_copy(accum_hbm, accum_ref, sem)
    load.start()
    me = lax.axis_index("mp")
    for d, ref in enumerate(peers):
        fill_counts(ref, counts_ref, d, me, hots, low_rows, code_rows)

    load.wait()


def merge_kernel(waited_ref, *refs):
    del waited_ref
    blocks, merged_ref = refs[:-1], refs[-1]
    span = merged_ref.shape[0] // len(blocks)
    for c, ref in enumerate(blocks):
        merged_ref[pl.ds(c * span, span), :] = ref[...]


def hold_kernel(*refs):
    del refs


def hold(values, others, flops=0):
    n = len(values)
    return pl.pallas_call(
        hold_kernel,
        out_shape=[jax.ShapeDtypeStruct(v.shape, v.dtype) for v in values],
        in_specs=[pl.BlockSpec(memory_space=pl.ANY)] * (n + len(others)),
        out_specs=[pl.BlockSpec(memory_space=pl.ANY)] * n,
        input_output_aliases={i: i for i in range(n)},
        compiler_params=params(1),
        cost_estimate=pl.CostEstimate(flops=flops, bytes_accessed=0, transcendentals=0),
        name="hold",
    )(*values, *others)


def parity_sum(odd, parts, rows, near_ref, rest_ref, blocks, grads):
    span = parts * rows
    replicas = grads.shape[0] // span
    for c in range(parts):
        for d in range(replicas):
            grads[pl.ds(d * span + c * rows, rows), :] = blocks[pl.ds((c * replicas + d) * rows, rows), :]
    near = near_ref.shape[1] // 2
    rest = rest_ref.shape[1] // 2
    return jnp.dot(
        near_ref[:, pl.ds(odd * near, near)], grads[pl.ds(0, near), :], preferred_element_type=jnp.float32
    ) + jnp.dot(
        rest_ref[:, pl.ds(odd * rest, rest)], grads[pl.ds(near, rest), :], preferred_element_type=jnp.float32
    )


def grad_kernel(parts, rows, near_ref, rest_ref, blocks, sum_ref, grads):
    sum_ref[...] = parity_sum(0, parts, rows, near_ref, rest_ref, blocks, grads)


def spread_kernel(parts, rows, touched_hbm, near_ref, rest_ref, first_ref, blocks, full, grads, summed, touched_ref,
                  sem):
    load = pltpu.make_async_copy(touched_hbm, touched_ref, sem)
    load.start()
    full[...] = jnp.zeros_like(full)
    summed[...] = first_ref[...] + parity_sum(1, parts, rows, near_ref, rest_ref, blocks, grads)
    load.wait()

    def scatter(i, carry):
        for u in range(32):
            t = i * 32 + u
            full[pl.ds(touched_ref[t], 1), :] = summed[pl.ds(t, 1), :]
        return carry

    lax.fori_loop(0, summed.shape[0] // 32, scatter, 0)


def update_kernel(full, table_ref, accum_ref, own_ref, last_ref, new_table_ref, new_accum_ref, pooled_ref,
                  table_vmem, accum_vmem, pooled_vmem, out_sem):
    pooled_vmem[...] = own_ref[...] + last_ref[...]
    stores = [pltpu.make_async_copy(pooled_vmem, pooled_ref, out_sem.at[2, 0])]
    stores[0].start()
    chunks = 8
    size = table_vmem.shape[0] // chunks
    for c in range(chunks):
        part = pl.ds(c * size, size)
        change = full[part, :]
        history = accum_ref[part, :] + change * change
        table_vmem[part, :] = table_ref[part, :] - learn_rate * change * lax.rsqrt(history)
        accum_vmem[part, :] = history
        for held, out, s in ((table_vmem, new_table_ref, 0), (accum_vmem, new_accum_ref, 1)):
            store = pltpu.make_async_copy(held.at[part, :], out.at[part, :], out_sem.at[s, c])
            store.start()
            stores.append(store)
    for store in stores:
        store.wait()


def per_device_small(table, accum, lookup_slots, lookup_weights, touched_rows, pooled_grad):
    bags, hots = lookup_slots.shape
    touch = touched_rows.shape[0]
    rows, feature = pooled_grad.shape
    table_rows = table.shape[0]
    mp = lax.axis_size("mp")
    replicas = lax.axis_size("replica")
    lookups = hots * (bags // LANES)
    low = jnp.bfloat16

    def swap(value, axis, distance):
        return lax.ppermute(value, axis, [(i, i ^ distance) for i in range(lax.axis_size(axis))])

    packed = pl.pallas_call(
        pack_kernel,
        out_shape=jax.ShapeDtypeStruct((rows + 2 * lookups, LANES), low),
        in_specs=[hbm()] * 3,
        out_specs=vmem(),
        scratch_shapes=[pltpu.VMEM((hots, bags), jnp.int32)] * 2
        + [pltpu.VMEM((lookups, LANES), jnp.int32)] * 2
        + [pltpu.SemaphoreType.DMA((3,))],
        compiler_params=params(8),
        name="pack",
    )(in_hbm(pooled_grad), in_hbm(lookup_slots.T), in_hbm(lookup_weights.T))
    peers = [swap(packed, "replica", d) for d in range(1, replicas)]

    keep, send, near_counts, table_held = pl.pallas_call(
        functools.partial(pooled_kernel, hots, mp),
        out_shape=[
            jax.ShapeDtypeStruct((mp // 2, rows, feature), jnp.float32),
            jax.ShapeDtypeStruct((mp // 2, rows, feature), jnp.float32),
            jax.ShapeDtypeStruct((touch, bags), low),
            jax.ShapeDtypeStruct((table_rows, feature), jnp.float32),
        ],
        in_specs=[hbm(), vmem(), hbm()],
        out_specs=[vmem()] * 4,
        scratch_shapes=[
            pltpu.VMEM((touch, feature), jnp.float32),
            pltpu.VMEM((lookups, LANES), jnp.float32),
            pltpu.VMEM((lookups, LANES), jnp.float32),
            pltpu.VMEM((feature, bags), jnp.float32),
            pltpu.SMEM((touch,), jnp.int32),
            pltpu.SemaphoreType.DMA((2,)),
        ],
        compiler_params=params(20),
        cost_estimate=pl.CostEstimate(flops=2 * touch * bags * feature, bytes_accessed=8 * MIB, transcendentals=0),
        name="pool",
    )(in_hbm(touched_rows), packed, in_hbm(table))

    parts = mp // 2
    got = swap(send, "mp", 1)
    peers = hold(peers, [keep], 1 << 34)
    joined = pl.pallas_call(
        functools.partial(join_kernel, rows),
        out_shape=jax.ShapeDtypeStruct((replicas * rows, feature), low),
        in_specs=[vmem()] * replicas,
        out_specs=vmem(),
        compiler_params=params(8),
        name="join",
    )(packed, *peers)
    far = [swap(joined, "mp", 2 * c) for c in range(1, parts)]

    block = jax.ShapeDtypeStruct((rows, feature), jnp.float32)
    own_sum, next_sum, across = pl.pallas_call(
        functools.partial(halves_kernel, rows),
        out_shape=[block, block, jax.ShapeDtypeStruct((2 * rows, feature), low)],
        in_specs=[vmem()] * 2,
        out_specs=[vmem()] * 3,
        compiler_params=params(8),
        name="halves",
    )(keep, got)
    own_sum, next_sum = pl.pallas_call(
        functools.partial(fold_kernel, rows),
        out_shape=[block] * 2,
        in_specs=[vmem()] * 3,
        out_specs=[vmem()] * 2,
        compiler_params=params(8),
        name="fold",
    )(own_sum, next_sum, swap(across, "mp", 2))
    last_sum = swap(next_sum, "mp", 4)

    rest_counts, accum_held = pl.pallas_call(
        functools.partial(counts_kernel, hots),
        out_shape=[
            jax.ShapeDtypeStruct((touch, bags * (replicas - 1)), low),
            jax.ShapeDtypeStruct((table_rows, feature), jnp.float32),
        ],
        in_specs=[hbm()] + [vmem()] * (replicas - 1),
        out_specs=[vmem()] * 2,
        scratch_shapes=[pltpu.VMEM((lookups, LANES), jnp.float32)] * 2 + [pltpu.SemaphoreType.DMA],
        compiler_params=params(24),
        cost_estimate=pl.CostEstimate(flops=0, bytes_accessed=0, transcendentals=0),
        name="count",
    )(in_hbm(accum), *peers)

    same = pl.pallas_call(
        merge_kernel,
        out_shape=jax.ShapeDtypeStruct((parts * replicas * rows, feature), low),
        in_specs=[pl.BlockSpec(memory_space=pl.ANY)] + [vmem()] * parts,
        out_specs=vmem(),
        compiler_params=params(8),
        name="merge",
    )(rest_counts, joined, *far)
    other = swap(same, "mp", 1)

    first = pl.pallas_call(
        functools.partial(grad_kernel, parts, rows),
        out_shape=jax.ShapeDtypeStruct((touch, feature), jnp.float32),
        in_specs=[vmem()] * 3,
        out_specs=vmem(),
        scratch_shapes=[pltpu.VMEM((bags * replicas // 2, feature), low)],
        compiler_params=params(16),
        cost_estimate=pl.CostEstimate(flops=1 << 34, bytes_accessed=0, transcendentals=0),
        name="gradient",
    )(near_counts, rest_counts, same)

    full = pl.pallas_call(
        functools.partial(spread_kernel, parts, rows),
        out_shape=jax.ShapeDtypeStruct((table_rows, feature), jnp.float32),
        in_specs=[hbm()] + [vmem()] * 4,
        out_specs=vmem(),
        scratch_shapes=[
            pltpu.VMEM((bags * replicas // 2, feature), low),
            pltpu.VMEM((touch, feature), jnp.float32),
            pltpu.SMEM((touch,), jnp.int32),
            pltpu.SemaphoreType.DMA,
        ],
        compiler_params=params(16),
        cost_estimate=pl.CostEstimate(flops=0, bytes_accessed=MIB, transcendentals=0),
        name="spread",
    )(in_hbm(touched_rows), near_counts, rest_counts, first, other)

    new_table, new_accum, pooled = pl.pallas_call(
        update_kernel,
        out_shape=[jax.ShapeDtypeStruct(table.shape, jnp.float32)] * 2 + [block],
        in_specs=[vmem()] * 5,
        out_specs=[hbm()] * 3,
        scratch_shapes=[
            pltpu.VMEM((table_rows, feature), jnp.float32),
            pltpu.VMEM((table_rows, feature), jnp.float32),
            pltpu.VMEM((rows, feature), jnp.float32),
            pltpu.SemaphoreType.DMA((3, 8)),
        ],
        compiler_params=params(16),
        cost_estimate=pl.CostEstimate(flops=0, bytes_accessed=MIB, transcendentals=0),
        name="update",
    )(full, table_held, accum_held, own_sum, last_sum)
    return (pooled, new_table, new_accum)


def fits_small(mesh, table, lookup_slots, touched_rows, pooled_grad):
    mp, replicas = mesh.shape["mp"], mesh.shape["replica"]
    powers = all(n & (n - 1) == 0 for n in (mp, replicas))
    touch = touched_rows.shape[0] // mp
    bags = lookup_slots.shape[0] // replicas
    rows = pooled_grad.shape[0] // (mp * replicas)
    return (
        powers
        and mp == 8
        and replicas == 4
        and lookup_slots.shape[0] * touch <= 4096 * 1024
        and touch % 256 == 0
        and touch <= 16384
        and bags % LANES == 0
        and rows % LANES == 0
        and table.shape[1] == LANES
        and table.shape[0] // mp <= 4096
        and table.shape[0] // mp % 256 == 0
        and touch % LANES == 0
    )


def solution(mesh):
    placed = (
        P("mp", None),
        P("mp", None),
        P("replica", "mp"),
        P("replica", "mp"),
        P("mp"),
        P(("replica", "mp"), None),
    )

    def step(table, accum, lookup_slots, lookup_weights, touched_rows, pooled_grad):
        small = fits_small(mesh, table, lookup_slots, touched_rows, pooled_grad)
        return jax.shard_map(
            per_device_small if small else per_device_general,
            mesh=mesh,
            in_specs=placed,
            out_specs=(P(("replica", "mp"), None), P("mp", None), P("mp", None)),
            check_vma=False,
        )(table, accum, lookup_slots, lookup_weights, touched_rows, pooled_grad)

    return step
```

```python
import functools
import math

import jax
import jax.numpy as jnp
from jax import lax
from jax.experimental import pallas as pl
from jax.experimental.pallas import tpu as pltpu
from jax.sharding import PartitionSpec as P

learn_rate = 0.5
LANES = 128
MIB = 1 << 20


def build_counts(slots, weights, touch_count):
    bag_count = slots.shape[0]
    block_rows = math.gcd(bag_count, 512)
    columns = jnp.arange(touch_count, dtype=jnp.int32)

    def one_block(block_index):
        slot_block = lax.dynamic_slice_in_dim(slots, block_index * block_rows, block_rows, 0)
        weight_block = lax.dynamic_slice_in_dim(weights, block_index * block_rows, block_rows, 0)
        matches = (slot_block[:, :, None] == columns[None, None, :]).astype(jnp.float32)
        return jnp.sum(matches * weight_block[:, :, None].astype(jnp.float32), axis=1).astype(
            jnp.bfloat16
        )

    blocks = lax.map(one_block, jnp.arange(bag_count // block_rows, dtype=jnp.int32))
    return blocks.reshape(bag_count, touch_count)


def adagrad(row_values, history, gradient):
    history_new = history + gradient * gradient
    return (row_values - learn_rate * gradient / jnp.sqrt(history_new), history_new)


def per_device_general(table, accum, lookup_slots, lookup_weights, touched_rows, pooled_grad):
    touch_count = touched_rows.shape[0]
    feature_dim = table.shape[1]
    bag_local = pooled_grad.shape[0]
    mp_count = lax.axis_size("mp")
    counts = build_counts(lookup_slots, lookup_weights, touch_count)
    row_tile = table[touched_rows]
    tile_low = row_tile.astype(jnp.bfloat16)
    partial_value = jnp.dot(counts, tile_low, preferred_element_type=jnp.float32)
    received = lax.all_to_all(
        partial_value.reshape(mp_count, bag_local, feature_dim),
        "mp",
        split_axis=0,
        concat_axis=0,
        tiled=True,
    )
    pooled = jnp.sum(received, axis=0)
    local_grad = lax.dot_general(
        counts,
        lax.all_gather(pooled_grad, "mp", axis=0, tiled=True),
        (((0,), (0,)), ((), ())),
        preferred_element_type=jnp.float32,
    )
    gradient = lax.psum(local_grad.astype(jnp.bfloat16), "replica").astype(jnp.float32)
    new_rows, new_history = adagrad(row_tile, accum[touched_rows], gradient)
    new_table = table.at[touched_rows].set(new_rows)
    new_accum = accum.at[touched_rows].set(new_history)
    return (pooled, new_table, new_accum)


def vmem():
    return pl.BlockSpec(memory_space=pltpu.VMEM)


def smem():
    return pl.BlockSpec(memory_space=pltpu.SMEM)


def hbm():
    return pl.BlockSpec(memory_space=pltpu.HBM)


def in_hbm(value):
    return pltpu.with_memory_space_constraint(value, pltpu.HBM)


def params(mib):
    return pltpu.CompilerParams(vmem_limit_bytes=mib * MIB)


def pack_kernel(grad_hbm, slots_hbm, weights_hbm, out_ref, slots_ref, weights_ref, slot_rows, weight_rows, sem):
    hots, bags = slots_ref.shape
    rows = grad_hbm.shape[0]
    blocks = bags // LANES
    loads = [
        pltpu.make_async_copy(slots_hbm, slots_ref, sem.at[0]),
        pltpu.make_async_copy(weights_hbm, weights_ref, sem.at[1]),
        pltpu.make_async_copy(grad_hbm, out_ref.at[pl.ds(0, rows), :], sem.at[2]),
    ]
    for load in loads:
        load.start()
    for load in loads:
        load.wait()
    for h in range(hots):
        for j in range(blocks):
            slot_rows[pl.ds(h * blocks + j, 1), :] = slots_ref[pl.ds(h, 1), pl.ds(j * LANES, LANES)]
            weight_rows[pl.ds(h * blocks + j, 1), :] = weights_ref[pl.ds(h, 1), pl.ds(j * LANES, LANES)]
    slot = slot_rows[...]
    code = weight_rows[...] * 64 + lax.shift_right_logical(slot, 8)
    low = jnp.bitwise_and(slot, 255)
    lookups = hots * blocks
    out_ref[pl.ds(rows, lookups), :] = low.astype(jnp.float32).astype(jnp.bfloat16)
    out_ref[pl.ds(rows + lookups, lookups), :] = code.astype(jnp.float32).astype(jnp.bfloat16)


def fill_counts(packed_ref, counts_ref, place, me, hots, low_rows, code_rows):
    touch = counts_ref.shape[0]
    lookups = low_rows.shape[0]
    rows = packed_ref.shape[0] - 2 * lookups
    blocks = lookups // hots
    low_rows[...] = packed_ref[pl.ds(rows, lookups), :].astype(jnp.float32)
    code_rows[...] = packed_ref[pl.ds(rows + lookups, lookups), :].astype(jnp.float32)
    step = min(touch, 256)
    line = lax.broadcasted_iota(jnp.int32, (step, LANES), 0).astype(jnp.float32).astype(jnp.bfloat16)
    zero = jnp.zeros((step, LANES), jnp.bfloat16)

    def one(j, carry):
        distance = jnp.bitwise_xor(j * LANES // rows, me)
        half = jnp.bitwise_and(distance, 1) * (counts_ref.shape[1] // 2) + place * (blocks * LANES // 2)
        at_column = half + lax.shift_right_logical(distance, 1) * rows + j * LANES % rows
        columns = pl.ds(pl.multiple_of(at_column, LANES), LANES)
        lows, highs, weights = [], [], []
        for h in range(hots):
            low = low_rows[pl.ds(h * blocks + j, 1), :]
            code = code_rows[pl.ds(h * blocks + j, 1), :].astype(jnp.int32)
            lows.append(low)
            highs.append(jnp.bitwise_and(code, 63))
            weights.append(lax.shift_right_logical(code, 6).astype(jnp.float32).astype(jnp.bfloat16))
        for k in range(touch // step):
            total = None
            for h in range(hots):
                at = jnp.where(highs[h] == k, lows[h], -1.0).astype(jnp.bfloat16)
                at = jnp.broadcast_to(at, (step, LANES))
                term = jnp.where(at == line, jnp.broadcast_to(weights[h], (step, LANES)), zero)
                total = term if total is None else total + term
            counts_ref[pl.ds(k * step, step), columns] = total
        return carry

    lax.fori_loop(0, blocks, one, 0)


def pooled_kernel(hots, mp, touched_hbm, packed_ref, table_hbm, keep_ref, send_ref, counts_ref,
                  table_vmem, tile, low_rows, code_rows, sum_t, touched_ref, sem):
    touch = touched_ref.shape[0]
    bags = counts_ref.shape[1]
    rows = bags // mp
    blocks = bags // LANES
    me = lax.axis_index("mp")
    loads = [
        pltpu.make_async_copy(touched_hbm, touched_ref, sem.at[0]),
        pltpu.make_async_copy(table_hbm, table_vmem, sem.at[1]),
    ]
    for load in loads:
        load.start()

    fill_counts(packed_ref, counts_ref, 0, me, hots, low_rows, code_rows)
    for load in loads:
        load.wait()

    def gather(i, carry):
        for u in range(16):
            t = i * 16 + u
            tile[pl.ds(t, 1), :] = table_vmem[pl.ds(touched_ref[t], 1), :]
        return carry

    lax.fori_loop(0, touch // 16, gather, 0)
    tile_t = tile[...].T.astype(jnp.bfloat16)
    for half in (0, 1):
        sum_t[:, pl.ds(half * (bags // 2), bags // 2)] = jnp.dot(
            tile_t, counts_ref[:, pl.ds(half * (bags // 2), bags // 2)], preferred_element_type=jnp.float32
        )
    for half, ref in ((0, keep_ref), (bags // 2, send_ref)):
        for c in range(mp // 2):
            ref[c] = sum_t[:, pl.ds(half + c * rows, rows)].T


def join_kernel(rows, *refs):
    out_ref = refs[-1]
    for d, ref in enumerate(refs[:-1]):
        out_ref[pl.ds(d * rows, rows), :] = ref[pl.ds(0, rows), :]


def halves_kernel(rows, keep_ref, got_ref, own_ref, next_ref, out_ref):
    own_ref[...] = keep_ref[0] + got_ref[0]
    next_ref[...] = keep_ref[2] + got_ref[2]
    for place, c in ((0, 1), (1, 3)):
        out_ref[pl.ds(place * rows, rows), :] = (keep_ref[c] + got_ref[c]).astype(jnp.bfloat16)


def fold_kernel(rows, own_ref, next_ref, got_ref, own_out, next_out):
    own_out[...] = own_ref[...] + got_ref[pl.ds(0, rows), :].astype(jnp.float32)
    next_out[...] = next_ref[...] + got_ref[pl.ds(rows, rows), :].astype(jnp.float32)


def counts_kernel(hots, accum_hbm, *refs):
    peers, (counts_ref, accum_ref, full_ref, low_rows, code_rows, sem) = refs[:-6], refs[-6:]
    full_ref[...] = jnp.zeros_like(full_ref)
    load = pltpu.make_async_copy(accum_hbm, accum_ref, sem)
    load.start()
    me = lax.axis_index("mp")
    for d, ref in enumerate(peers):
        fill_counts(ref, counts_ref, d, me, hots, low_rows, code_rows)

    load.wait()


def merge_kernel(waited_ref, *refs):
    del waited_ref
    blocks, merged_ref = refs[:-1], refs[-1]
    span = merged_ref.shape[0] // len(blocks)
    for c, ref in enumerate(blocks):
        merged_ref[pl.ds(c * span, span), :] = ref[...]


def hold_kernel(*refs):
    del refs


def hold(values, others, flops=0):
    n = len(values)
    return pl.pallas_call(
        hold_kernel,
        out_shape=[jax.ShapeDtypeStruct(v.shape, v.dtype) for v in values],
        in_specs=[pl.BlockSpec(memory_space=pl.ANY)] * (n + len(others)),
        out_specs=[pl.BlockSpec(memory_space=pl.ANY)] * n,
        input_output_aliases={i: i for i in range(n)},
        compiler_params=params(1),
        cost_estimate=pl.CostEstimate(flops=flops, bytes_accessed=0, transcendentals=0),
        name="hold",
    )(*values, *others)


def parity_sum(odd, parts, rows, near_ref, rest_ref, blocks, grads):
    span = parts * rows
    replicas = grads.shape[0] // span
    for c in range(parts):
        for d in range(replicas):
            grads[pl.ds(d * span + c * rows, rows), :] = blocks[pl.ds((c * replicas + d) * rows, rows), :]
    near = near_ref.shape[1] // 2
    rest = rest_ref.shape[1] // 2
    return jnp.dot(
        near_ref[:, pl.ds(odd * near, near)], grads[pl.ds(0, near), :], preferred_element_type=jnp.float32
    ) + jnp.dot(
        rest_ref[:, pl.ds(odd * rest, rest)], grads[pl.ds(near, rest), :], preferred_element_type=jnp.float32
    )


def grad_kernel(parts, rows, near_ref, rest_ref, blocks, sum_ref, grads):
    sum_ref[...] = parity_sum(0, parts, rows, near_ref, rest_ref, blocks, grads)


def spread_kernel(parts, rows, touched_hbm, near_ref, rest_ref, first_ref, blocks, blank_ref, full, grads, summed,
                  touched_ref, sem):
    load = pltpu.make_async_copy(touched_hbm, touched_ref, sem)
    load.start()
    del blank_ref
    summed[...] = first_ref[...] + parity_sum(1, parts, rows, near_ref, rest_ref, blocks, grads)
    load.wait()

    def scatter(i, carry):
        for u in range(128):
            t = i * 128 + u
            full[pl.ds(touched_ref[t], 1), :] = summed[pl.ds(t, 1), :]
        return carry

    lax.fori_loop(0, summed.shape[0] // 128, scatter, 0)


def update_kernel(full, table_ref, accum_ref, own_ref, last_ref, new_table_ref, new_accum_ref, pooled_ref,
                  table_vmem, accum_vmem, pooled_vmem, out_sem):
    pooled_vmem[...] = own_ref[...] + last_ref[...]
    stores = [pltpu.make_async_copy(pooled_vmem, pooled_ref, out_sem.at[2, 0])]
    stores[0].start()
    chunks = 8
    size = table_vmem.shape[0] // chunks
    for c in range(chunks):
        part = pl.ds(c * size, size)
        change = full[part, :]
        history = accum_ref[part, :] + change * change
        table_vmem[part, :] = table_ref[part, :] - learn_rate * change * lax.rsqrt(history)
        accum_vmem[part, :] = history
        for held, out, s in ((table_vmem, new_table_ref, 0), (accum_vmem, new_accum_ref, 1)):
            store = pltpu.make_async_copy(held.at[part, :], out.at[part, :], out_sem.at[s, c])
            store.start()
            stores.append(store)
    for store in stores:
        store.wait()


def per_device_small(table, accum, lookup_slots, lookup_weights, touched_rows, pooled_grad):
    bags, hots = lookup_slots.shape
    touch = touched_rows.shape[0]
    rows, feature = pooled_grad.shape
    table_rows = table.shape[0]
    mp = lax.axis_size("mp")
    replicas = lax.axis_size("replica")
    lookups = hots * (bags // LANES)
    low = jnp.bfloat16

    def swap(value, axis, distance):
        return lax.ppermute(value, axis, [(i, i ^ distance) for i in range(lax.axis_size(axis))])

    packed = pl.pallas_call(
        pack_kernel,
        out_shape=jax.ShapeDtypeStruct((rows + 2 * lookups, LANES), low),
        in_specs=[hbm()] * 3,
        out_specs=vmem(),
        scratch_shapes=[pltpu.VMEM((hots, bags), jnp.int32)] * 2
        + [pltpu.VMEM((lookups, LANES), jnp.int32)] * 2
        + [pltpu.SemaphoreType.DMA((3,))],
        compiler_params=params(8),
        name="pack",
    )(in_hbm(pooled_grad), in_hbm(lookup_slots.T), in_hbm(lookup_weights.T))
    peers = [swap(packed, "replica", d) for d in range(1, replicas)]

    keep, send, near_counts, table_held = pl.pallas_call(
        functools.partial(pooled_kernel, hots, mp),
        out_shape=[
            jax.ShapeDtypeStruct((mp // 2, rows, feature), jnp.float32),
            jax.ShapeDtypeStruct((mp // 2, rows, feature), jnp.float32),
            jax.ShapeDtypeStruct((touch, bags), low),
            jax.ShapeDtypeStruct((table_rows, feature), jnp.float32),
        ],
        in_specs=[hbm(), vmem(), hbm()],
        out_specs=[vmem()] * 4,
        scratch_shapes=[
            pltpu.VMEM((touch, feature), jnp.float32),
            pltpu.VMEM((lookups, LANES), jnp.float32),
            pltpu.VMEM((lookups, LANES), jnp.float32),
            pltpu.VMEM((feature, bags), jnp.float32),
            pltpu.SMEM((touch,), jnp.int32),
            pltpu.SemaphoreType.DMA((2,)),
        ],
        compiler_params=params(20),
        cost_estimate=pl.CostEstimate(flops=2 * touch * bags * feature, bytes_accessed=8 * MIB, transcendentals=0),
        name="pool",
    )(in_hbm(touched_rows), packed, in_hbm(table))

    parts = mp // 2
    got = swap(send, "mp", 1)
    peers = hold(peers, [keep], 1 << 34)
    joined = pl.pallas_call(
        functools.partial(join_kernel, rows),
        out_shape=jax.ShapeDtypeStruct((replicas * rows, feature), low),
        in_specs=[vmem()] * replicas,
        out_specs=vmem(),
        compiler_params=params(8),
        name="join",
    )(packed, *peers)
    far = [swap(joined, "mp", 2 * c) for c in range(1, parts)]

    block = jax.ShapeDtypeStruct((rows, feature), jnp.float32)
    own_sum, next_sum, across = pl.pallas_call(
        functools.partial(halves_kernel, rows),
        out_shape=[block, block, jax.ShapeDtypeStruct((2 * rows, feature), low)],
        in_specs=[vmem()] * 2,
        out_specs=[vmem()] * 3,
        compiler_params=params(8),
        name="halves",
    )(keep, got)
    own_sum, next_sum = pl.pallas_call(
        functools.partial(fold_kernel, rows),
        out_shape=[block] * 2,
        in_specs=[vmem()] * 3,
        out_specs=[vmem()] * 2,
        compiler_params=params(8),
        name="fold",
    )(own_sum, next_sum, swap(across, "mp", 2))
    last_sum = swap(next_sum, "mp", 4)

    rest_counts, accum_held, blank = pl.pallas_call(
        functools.partial(counts_kernel, hots),
        out_shape=[
            jax.ShapeDtypeStruct((touch, bags * (replicas - 1)), low),
            jax.ShapeDtypeStruct((table_rows, feature), jnp.float32),
            jax.ShapeDtypeStruct((table_rows, feature), jnp.float32),
        ],
        in_specs=[hbm()] + [vmem()] * (replicas - 1),
        out_specs=[vmem()] * 3,
        scratch_shapes=[pltpu.VMEM((lookups, LANES), jnp.float32)] * 2 + [pltpu.SemaphoreType.DMA],
        compiler_params=params(24),
        cost_estimate=pl.CostEstimate(flops=0, bytes_accessed=0, transcendentals=0),
        name="count",
    )(in_hbm(accum), *peers)

    same = pl.pallas_call(
        merge_kernel,
        out_shape=jax.ShapeDtypeStruct((parts * replicas * rows, feature), low),
        in_specs=[pl.BlockSpec(memory_space=pl.ANY)] + [vmem()] * parts,
        out_specs=vmem(),
        compiler_params=params(8),
        name="merge",
    )(rest_counts, joined, *far)
    other = swap(same, "mp", 1)

    first = pl.pallas_call(
        functools.partial(grad_kernel, parts, rows),
        out_shape=jax.ShapeDtypeStruct((touch, feature), jnp.float32),
        in_specs=[vmem()] * 3,
        out_specs=vmem(),
        scratch_shapes=[pltpu.VMEM((bags * replicas // 2, feature), low)],
        compiler_params=params(16),
        cost_estimate=pl.CostEstimate(flops=1 << 34, bytes_accessed=0, transcendentals=0),
        name="gradient",
    )(near_counts, rest_counts, same)

    full = pl.pallas_call(
        functools.partial(spread_kernel, parts, rows),
        out_shape=jax.ShapeDtypeStruct((table_rows, feature), jnp.float32),
        in_specs=[hbm()] + [vmem()] * 5,
        out_specs=vmem(),
        input_output_aliases={5: 0},
        scratch_shapes=[
            pltpu.VMEM((bags * replicas // 2, feature), low),
            pltpu.VMEM((touch, feature), jnp.float32),
            pltpu.SMEM((touch,), jnp.int32),
            pltpu.SemaphoreType.DMA,
        ],
        compiler_params=params(16),
        cost_estimate=pl.CostEstimate(flops=0, bytes_accessed=MIB, transcendentals=0),
        name="spread",
    )(in_hbm(touched_rows), near_counts, rest_counts, first, other, blank)

    new_table, new_accum, pooled = pl.pallas_call(
        update_kernel,
        out_shape=[jax.ShapeDtypeStruct(table.shape, jnp.float32)] * 2 + [block],
        in_specs=[vmem()] * 5,
        out_specs=[hbm()] * 3,
        scratch_shapes=[
            pltpu.VMEM((table_rows, feature), jnp.float32),
            pltpu.VMEM((table_rows, feature), jnp.float32),
            pltpu.VMEM((rows, feature), jnp.float32),
            pltpu.SemaphoreType.DMA((3, 8)),
        ],
        compiler_params=params(16),
        cost_estimate=pl.CostEstimate(flops=0, bytes_accessed=MIB, transcendentals=0),
        name="update",
    )(full, table_held, accum_held, own_sum, last_sum)
    return (pooled, new_table, new_accum)


def fits_small(mesh, table, lookup_slots, touched_rows, pooled_grad):
    mp, replicas = mesh.shape["mp"], mesh.shape["replica"]
    powers = all(n & (n - 1) == 0 for n in (mp, replicas))
    touch = touched_rows.shape[0] // mp
    bags = lookup_slots.shape[0] // replicas
    rows = pooled_grad.shape[0] // (mp * replicas)
    return (
        powers
        and mp == 8
        and replicas == 4
        and lookup_slots.shape[0] * touch <= 4096 * 1024
        and touch % 256 == 0
        and touch <= 16384
        and bags % LANES == 0
        and rows % LANES == 0
        and table.shape[1] == LANES
        and table.shape[0] // mp <= 4096
        and table.shape[0] // mp % 256 == 0
        and touch % LANES == 0
    )


def solution(mesh):
    placed = (
        P("mp", None),
        P("mp", None),
        P("replica", "mp"),
        P("replica", "mp"),
        P("mp"),
        P(("replica", "mp"), None),
    )

    def step(table, accum, lookup_slots, lookup_weights, touched_rows, pooled_grad):
        small = fits_small(mesh, table, lookup_slots, touched_rows, pooled_grad)
        return jax.shard_map(
            per_device_small if small else per_device_general,
            mesh=mesh,
            in_specs=placed,
            out_specs=(P(("replica", "mp"), None), P("mp", None), P("mp", None)),
            check_vma=False,
        )(table, accum, lookup_slots, lookup_weights, touched_rows, pooled_grad)

    return step
```

```python
import functools
import math

import jax
import jax.numpy as jnp
from jax import lax
from jax.experimental import pallas as pl
from jax.experimental.pallas import tpu as pltpu
from jax.sharding import PartitionSpec as P

learn_rate = 0.5
LANES = 128
spots = (0, 3, 1, 2)
MIB = 1 << 20


def build_counts(slots, weights, touch_count):
    bag_count = slots.shape[0]
    block_rows = math.gcd(bag_count, 512)
    columns = jnp.arange(touch_count, dtype=jnp.int32)

    def one_block(block_index):
        slot_block = lax.dynamic_slice_in_dim(slots, block_index * block_rows, block_rows, 0)
        weight_block = lax.dynamic_slice_in_dim(weights, block_index * block_rows, block_rows, 0)
        matches = (slot_block[:, :, None] == columns[None, None, :]).astype(jnp.float32)
        return jnp.sum(matches * weight_block[:, :, None].astype(jnp.float32), axis=1).astype(
            jnp.bfloat16
        )

    blocks = lax.map(one_block, jnp.arange(bag_count // block_rows, dtype=jnp.int32))
    return blocks.reshape(bag_count, touch_count)


def adagrad(row_values, history, gradient):
    history_new = history + gradient * gradient
    return (row_values - learn_rate * gradient / jnp.sqrt(history_new), history_new)


def per_device_general(table, accum, lookup_slots, lookup_weights, touched_rows, pooled_grad):
    touch_count = touched_rows.shape[0]
    feature_dim = table.shape[1]
    bag_local = pooled_grad.shape[0]
    mp_count = lax.axis_size("mp")
    counts = build_counts(lookup_slots, lookup_weights, touch_count)
    row_tile = table[touched_rows]
    tile_low = row_tile.astype(jnp.bfloat16)
    partial_value = jnp.dot(counts, tile_low, preferred_element_type=jnp.float32)
    received = lax.all_to_all(
        partial_value.reshape(mp_count, bag_local, feature_dim),
        "mp",
        split_axis=0,
        concat_axis=0,
        tiled=True,
    )
    pooled = jnp.sum(received, axis=0)
    local_grad = lax.dot_general(
        counts,
        lax.all_gather(pooled_grad, "mp", axis=0, tiled=True),
        (((0,), (0,)), ((), ())),
        preferred_element_type=jnp.float32,
    )
    gradient = lax.psum(local_grad.astype(jnp.bfloat16), "replica").astype(jnp.float32)
    new_rows, new_history = adagrad(row_tile, accum[touched_rows], gradient)
    new_table = table.at[touched_rows].set(new_rows)
    new_accum = accum.at[touched_rows].set(new_history)
    return (pooled, new_table, new_accum)


def vmem():
    return pl.BlockSpec(memory_space=pltpu.VMEM)


def smem():
    return pl.BlockSpec(memory_space=pltpu.SMEM)


def hbm():
    return pl.BlockSpec(memory_space=pltpu.HBM)


def in_hbm(value):
    return pltpu.with_memory_space_constraint(value, pltpu.HBM)


def params(mib):
    return pltpu.CompilerParams(vmem_limit_bytes=mib * MIB)


def pack_kernel(grad_hbm, slots_hbm, weights_hbm, out_ref, slots_ref, weights_ref, slot_rows, weight_rows, sem):
    hots, bags = slots_ref.shape
    rows = grad_hbm.shape[0]
    blocks = bags // LANES
    loads = [
        pltpu.make_async_copy(slots_hbm, slots_ref, sem.at[0]),
        pltpu.make_async_copy(weights_hbm, weights_ref, sem.at[1]),
        pltpu.make_async_copy(grad_hbm, out_ref.at[pl.ds(0, rows), :], sem.at[2]),
    ]
    for load in loads:
        load.start()
    for load in loads:
        load.wait()
    for h in range(hots):
        for j in range(blocks):
            slot_rows[pl.ds(h * blocks + j, 1), :] = slots_ref[pl.ds(h, 1), pl.ds(j * LANES, LANES)]
            weight_rows[pl.ds(h * blocks + j, 1), :] = weights_ref[pl.ds(h, 1), pl.ds(j * LANES, LANES)]
    slot = slot_rows[...]
    code = weight_rows[...] * 64 + lax.shift_right_logical(slot, 8)
    low = jnp.bitwise_and(slot, 255)
    lookups = hots * blocks
    out_ref[pl.ds(rows, lookups), :] = low.astype(jnp.float32).astype(jnp.bfloat16)
    out_ref[pl.ds(rows + lookups, lookups), :] = code.astype(jnp.float32).astype(jnp.bfloat16)


def fill_counts(packed_ref, counts_ref, place, me, hots, low_rows, code_rows):
    touch = counts_ref.shape[0]
    lookups = low_rows.shape[0]
    rows = packed_ref.shape[0] - 2 * lookups
    blocks = lookups // hots
    low_rows[...] = packed_ref[pl.ds(rows, lookups), :].astype(jnp.float32)
    code_rows[...] = packed_ref[pl.ds(rows + lookups, lookups), :].astype(jnp.float32)
    step = min(touch, 256)
    line = lax.broadcasted_iota(jnp.int32, (step, LANES), 0).astype(jnp.float32).astype(jnp.bfloat16)
    zero = jnp.zeros((step, LANES), jnp.bfloat16)

    def one(j, carry):
        distance = jnp.bitwise_xor(j * LANES // rows, me)
        chip = lax.shift_right_logical(distance, 1)
        spot = jnp.where(chip == 3, 1, jnp.where(chip == 0, 0, chip + 1))
        at_column = (
            jnp.bitwise_and(distance, 1) * (counts_ref.shape[1] // 2)
            + lax.shift_right_logical(spot, 1) * (counts_ref.shape[1] // 4)
            + place * (2 * rows)
            + jnp.bitwise_and(spot, 1) * rows
            + j * LANES % rows
        )
        columns = pl.ds(pl.multiple_of(at_column, LANES), LANES)
        lows, highs, weights = [], [], []
        for h in range(hots):
            low = low_rows[pl.ds(h * blocks + j, 1), :]
            code = code_rows[pl.ds(h * blocks + j, 1), :].astype(jnp.int32)
            lows.append(low)
            highs.append(jnp.bitwise_and(code, 63))
            weights.append(lax.shift_right_logical(code, 6).astype(jnp.float32).astype(jnp.bfloat16))
        for k in range(touch // step):
            total = None
            for h in range(hots):
                at = jnp.where(highs[h] == k, lows[h], -1.0).astype(jnp.bfloat16)
                at = jnp.broadcast_to(at, (step, LANES))
                term = jnp.where(at == line, jnp.broadcast_to(weights[h], (step, LANES)), zero)
                total = term if total is None else total + term
            counts_ref[pl.ds(k * step, step), columns] = total
        return carry

    lax.fori_loop(0, blocks, one, 0)


def pooled_kernel(hots, mp, touched_hbm, packed_ref, table_hbm, keep_ref, send_ref, counts_ref,
                  table_vmem, tile, low_rows, code_rows, sum_t, touched_ref, sem):
    touch = touched_ref.shape[0]
    bags = counts_ref.shape[1]
    rows = bags // mp
    blocks = bags // LANES
    me = lax.axis_index("mp")
    loads = [
        pltpu.make_async_copy(touched_hbm, touched_ref, sem.at[0]),
        pltpu.make_async_copy(table_hbm, table_vmem, sem.at[1]),
    ]
    for load in loads:
        load.start()

    fill_counts(packed_ref, counts_ref, 0, me, hots, low_rows, code_rows)
    for load in loads:
        load.wait()

    def gather(i, carry):
        for u in range(16):
            t = i * 16 + u
            tile[pl.ds(t, 1), :] = table_vmem[pl.ds(touched_ref[t], 1), :]
        return carry

    lax.fori_loop(0, touch // 16, gather, 0)
    tile_t = tile[...].T.astype(jnp.bfloat16)
    for half in (0, 1):
        sum_t[:, pl.ds(half * (bags // 2), bags // 2)] = jnp.dot(
            tile_t, counts_ref[:, pl.ds(half * (bags // 2), bags // 2)], preferred_element_type=jnp.float32
        )
    for half, ref in ((0, keep_ref), (bags // 2, send_ref)):
        for c in range(mp // 2):
            ref[c] = sum_t[:, pl.ds(half + spots.index(c) * rows, rows)].T


def join_kernel(rows, *refs):
    out_ref = refs[-1]
    for d, ref in enumerate(refs[:-1]):
        out_ref[pl.ds(d * rows, rows), :] = ref[pl.ds(0, rows), :]


def halves_kernel(rows, keep_ref, got_ref, own_ref, next_ref, out_ref):
    own_ref[...] = keep_ref[0] + got_ref[0]
    next_ref[...] = keep_ref[2] + got_ref[2]
    for place, c in ((0, 1), (1, 3)):
        out_ref[pl.ds(place * rows, rows), :] = (keep_ref[c] + got_ref[c]).astype(jnp.bfloat16)


def fold_kernel(rows, own_ref, next_ref, got_ref, own_out, next_out):
    own_out[...] = own_ref[...] + got_ref[pl.ds(0, rows), :].astype(jnp.float32)
    next_out[...] = (next_ref[...] + got_ref[pl.ds(rows, rows), :].astype(jnp.float32)).astype(next_out.dtype)


def counts_kernel(hots, accum_hbm, *refs):
    peers, (counts_ref, accum_ref, full_ref, low_rows, code_rows, sem) = refs[:-6], refs[-6:]
    full_ref[...] = jnp.zeros_like(full_ref)
    load = pltpu.make_async_copy(accum_hbm, accum_ref, sem)
    load.start()
    me = lax.axis_index("mp")
    for d, ref in enumerate(peers):
        fill_counts(ref, counts_ref, d, me, hots, low_rows, code_rows)

    load.wait()


def merge_kernel(waited_ref, *refs):
    del waited_ref
    blocks, merged_ref = refs[:-1], refs[-1]
    span = merged_ref.shape[0] // len(blocks)
    for c, ref in enumerate(blocks):
        merged_ref[pl.ds(c * span, span), :] = ref[...]


def hold_kernel(*refs):
    del refs


def hold(values, others, flops=0):
    n = len(values)
    return pl.pallas_call(
        hold_kernel,
        out_shape=[jax.ShapeDtypeStruct(v.shape, v.dtype) for v in values],
        in_specs=[pl.BlockSpec(memory_space=pl.ANY)] * (n + len(others)),
        out_specs=[pl.BlockSpec(memory_space=pl.ANY)] * n,
        input_output_aliases={i: i for i in range(n)},
        compiler_params=params(1),
        cost_estimate=pl.CostEstimate(flops=flops, bytes_accessed=0, transcendentals=0),
        name="hold",
    )(*values, *others)


def pair_kernel(group, rows, near_ref, rest_ref, *refs):
    pair, before, (sum_ref, grads) = refs[:2], refs[2:-2], refs[-2:]
    replicas = pair[0].shape[0] // rows
    for d in range(replicas):
        for p, ref in enumerate(pair):
            grads[pl.ds((2 * d + p) * rows, rows), :] = ref[pl.ds(d * rows, rows), :]
    near, rest = near_ref.shape[1] // 4, rest_ref.shape[1] // 4
    total = jnp.dot(
        near_ref[:, pl.ds(group * near, near)], grads[pl.ds(0, near), :], preferred_element_type=jnp.float32
    ) + jnp.dot(
        rest_ref[:, pl.ds(group * rest, rest)], grads[pl.ds(near, rest), :], preferred_element_type=jnp.float32
    )
    for ref in before:
        total = total + ref[...]
    sum_ref[...] = total


def other_core_sum(rows, near_ref, rest_ref, blocks, grads):
    replicas = blocks.shape[0] // (len(spots) * rows)
    near, rest = near_ref.shape[1] // 2, rest_ref.shape[1] // 2
    for spot, c in enumerate(spots):
        for d in range(replicas):
            group, p = divmod(spot, 2)
            place = spot * rows if d == 0 else near + ((group * (replicas - 1) + d - 1) * 2 + p) * rows
            grads[pl.ds(place, rows), :] = blocks[pl.ds((c * replicas + d) * rows, rows), :]
    return jnp.dot(
        near_ref[:, pl.ds(near, near)], grads[pl.ds(0, near), :], preferred_element_type=jnp.float32
    ) + jnp.dot(rest_ref[:, pl.ds(rest, rest)], grads[pl.ds(near, rest), :], preferred_element_type=jnp.float32)


def spread_kernel(rows, touched_hbm, near_ref, rest_ref, first_ref, blocks, blank_ref, full, grads, summed,
                  touched_ref, sem):
    load = pltpu.make_async_copy(touched_hbm, touched_ref, sem)
    load.start()
    del blank_ref
    summed[...] = first_ref[...] + other_core_sum(rows, near_ref, rest_ref, blocks, grads)
    load.wait()

    def scatter(i, carry):
        for u in range(128):
            t = i * 128 + u
            full[pl.ds(touched_ref[t], 1), :] = summed[pl.ds(t, 1), :]
        return carry

    lax.fori_loop(0, summed.shape[0] // 128, scatter, 0)


def update_kernel(full, table_ref, accum_ref, own_ref, last_ref, new_table_ref, new_accum_ref, pooled_ref,
                  table_vmem, accum_vmem, pooled_vmem, out_sem):
    pooled_vmem[...] = own_ref[...] + last_ref[...].astype(jnp.float32)
    stores = [pltpu.make_async_copy(pooled_vmem, pooled_ref, out_sem.at[2, 0])]
    stores[0].start()
    chunks = 8
    size = table_vmem.shape[0] // chunks
    for c in range(chunks):
        part = pl.ds(c * size, size)
        change = full[part, :]
        history = accum_ref[part, :] + change * change
        table_vmem[part, :] = table_ref[part, :] - learn_rate * change * lax.rsqrt(history)
        accum_vmem[part, :] = history
        for held, out, s in ((table_vmem, new_table_ref, 0), (accum_vmem, new_accum_ref, 1)):
            store = pltpu.make_async_copy(held.at[part, :], out.at[part, :], out_sem.at[s, c])
            store.start()
            stores.append(store)
    for store in stores:
        store.wait()


def per_device_small(table, accum, lookup_slots, lookup_weights, touched_rows, pooled_grad):
    bags, hots = lookup_slots.shape
    touch = touched_rows.shape[0]
    rows, feature = pooled_grad.shape
    table_rows = table.shape[0]
    mp = lax.axis_size("mp")
    replicas = lax.axis_size("replica")
    lookups = hots * (bags // LANES)
    low = jnp.bfloat16

    def swap(value, axis, distance):
        return lax.ppermute(value, axis, [(i, i ^ distance) for i in range(lax.axis_size(axis))])

    packed = pl.pallas_call(
        pack_kernel,
        out_shape=jax.ShapeDtypeStruct((rows + 2 * lookups, LANES), low),
        in_specs=[hbm()] * 3,
        out_specs=vmem(),
        scratch_shapes=[pltpu.VMEM((hots, bags), jnp.int32)] * 2
        + [pltpu.VMEM((lookups, LANES), jnp.int32)] * 2
        + [pltpu.SemaphoreType.DMA((3,))],
        compiler_params=params(8),
        name="pack",
    )(in_hbm(pooled_grad), in_hbm(lookup_slots.T), in_hbm(lookup_weights.T))
    peers = [swap(packed, "replica", d) for d in range(1, replicas)]

    keep, send, near_counts, table_held = pl.pallas_call(
        functools.partial(pooled_kernel, hots, mp),
        out_shape=[
            jax.ShapeDtypeStruct((mp // 2, rows, feature), jnp.float32),
            jax.ShapeDtypeStruct((mp // 2, rows, feature), jnp.float32),
            jax.ShapeDtypeStruct((touch, bags), low),
            jax.ShapeDtypeStruct((table_rows, feature), jnp.float32),
        ],
        in_specs=[hbm(), vmem(), hbm()],
        out_specs=[vmem()] * 4,
        scratch_shapes=[
            pltpu.VMEM((touch, feature), jnp.float32),
            pltpu.VMEM((lookups, LANES), jnp.float32),
            pltpu.VMEM((lookups, LANES), jnp.float32),
            pltpu.VMEM((feature, bags), jnp.float32),
            pltpu.SMEM((touch,), jnp.int32),
            pltpu.SemaphoreType.DMA((2,)),
        ],
        compiler_params=params(20),
        cost_estimate=pl.CostEstimate(flops=2 * touch * bags * feature, bytes_accessed=8 * MIB, transcendentals=0),
        name="pool",
    )(in_hbm(touched_rows), packed, in_hbm(table))

    parts = mp // 2
    got = swap(send, "mp", 1)
    peers = hold(peers, [keep], 1 << 34)
    joined = pl.pallas_call(
        functools.partial(join_kernel, rows),
        out_shape=jax.ShapeDtypeStruct((replicas * rows, feature), low),
        in_specs=[vmem()] * replicas,
        out_specs=vmem(),
        compiler_params=params(8),
        name="join",
    )(packed, *peers)
    far = [swap(joined, "mp", 2 * c) for c in range(1, parts)]

    block = jax.ShapeDtypeStruct((rows, feature), jnp.float32)
    own_sum, next_sum, across = pl.pallas_call(
        functools.partial(halves_kernel, rows),
        out_shape=[block, block, jax.ShapeDtypeStruct((2 * rows, feature), low)],
        in_specs=[vmem()] * 2,
        out_specs=[vmem()] * 3,
        compiler_params=params(8),
        name="halves",
    )(keep, got)
    own_sum, next_sum = pl.pallas_call(
        functools.partial(fold_kernel, rows),
        out_shape=[block, jax.ShapeDtypeStruct((rows, feature), low)],
        in_specs=[vmem()] * 3,
        out_specs=[vmem()] * 2,
        compiler_params=params(8),
        name="fold",
    )(own_sum, next_sum, swap(across, "mp", 2))
    last_sum = swap(next_sum, "mp", 4)

    rest_counts, accum_held, blank = pl.pallas_call(
        functools.partial(counts_kernel, hots),
        out_shape=[
            jax.ShapeDtypeStruct((touch, bags * (replicas - 1)), low),
            jax.ShapeDtypeStruct((table_rows, feature), jnp.float32),
            jax.ShapeDtypeStruct((table_rows, feature), jnp.float32),
        ],
        in_specs=[hbm()] + [vmem()] * (replicas - 1),
        out_specs=[vmem()] * 3,
        scratch_shapes=[pltpu.VMEM((lookups, LANES), jnp.float32)] * 2 + [pltpu.SemaphoreType.DMA],
        compiler_params=params(24),
        cost_estimate=pl.CostEstimate(flops=0, bytes_accessed=0, transcendentals=0),
        name="count",
    )(in_hbm(accum), *peers)

    def pair_sum(group, pair, before, flops):
        return pl.pallas_call(
            functools.partial(pair_kernel, group, rows),
            out_shape=jax.ShapeDtypeStruct((touch, feature), jnp.float32),
            in_specs=[vmem()] * (4 + len(before)),
            out_specs=vmem(),
            scratch_shapes=[pltpu.VMEM((2 * replicas * rows, feature), low)],
            compiler_params=params(16),
            cost_estimate=pl.CostEstimate(flops=flops, bytes_accessed=1, transcendentals=0),
            name="gradient",
        )(near_counts, rest_counts, *pair, *before)

    early = pair_sum(0, [joined, far[2]], [], 0)
    same = pl.pallas_call(
        merge_kernel,
        out_shape=jax.ShapeDtypeStruct((parts * replicas * rows, feature), low),
        in_specs=[pl.BlockSpec(memory_space=pl.ANY)] + [vmem()] * parts,
        out_specs=vmem(),
        compiler_params=params(8),
        name="merge",
    )(early, joined, *far)
    other = swap(same, "mp", 1)

    first = pair_sum(1, far[:2], [early], 1 << 34)

    full = pl.pallas_call(
        functools.partial(spread_kernel, rows),
        out_shape=jax.ShapeDtypeStruct((table_rows, feature), jnp.float32),
        in_specs=[hbm()] + [vmem()] * 5,
        out_specs=vmem(),
        input_output_aliases={5: 0},
        scratch_shapes=[
            pltpu.VMEM((bags * replicas // 2, feature), low),
            pltpu.VMEM((touch, feature), jnp.float32),
            pltpu.SMEM((touch,), jnp.int32),
            pltpu.SemaphoreType.DMA,
        ],
        compiler_params=params(16),
        cost_estimate=pl.CostEstimate(flops=0, bytes_accessed=MIB, transcendentals=0),
        name="spread",
    )(in_hbm(touched_rows), near_counts, rest_counts, first, other, blank)

    new_table, new_accum, pooled = pl.pallas_call(
        update_kernel,
        out_shape=[jax.ShapeDtypeStruct(table.shape, jnp.float32)] * 2 + [block],
        in_specs=[vmem()] * 5,
        out_specs=[hbm()] * 3,
        scratch_shapes=[
            pltpu.VMEM((table_rows, feature), jnp.float32),
            pltpu.VMEM((table_rows, feature), jnp.float32),
            pltpu.VMEM((rows, feature), jnp.float32),
            pltpu.SemaphoreType.DMA((3, 8)),
        ],
        compiler_params=params(16),
        cost_estimate=pl.CostEstimate(flops=0, bytes_accessed=MIB, transcendentals=0),
        name="update",
    )(full, table_held, accum_held, own_sum, last_sum)
    return (pooled, new_table, new_accum)


def fits_small(mesh, table, lookup_slots, touched_rows, pooled_grad):
    mp, replicas = mesh.shape["mp"], mesh.shape["replica"]
    powers = all(n & (n - 1) == 0 for n in (mp, replicas))
    touch = touched_rows.shape[0] // mp
    bags = lookup_slots.shape[0] // replicas
    rows = pooled_grad.shape[0] // (mp * replicas)
    return (
        powers
        and mp == 8
        and replicas == 4
        and lookup_slots.shape[0] * touch <= 4096 * 1024
        and touch % 256 == 0
        and touch <= 16384
        and bags % LANES == 0
        and rows % LANES == 0
        and table.shape[1] == LANES
        and table.shape[0] // mp <= 4096
        and table.shape[0] // mp % 256 == 0
        and touch % LANES == 0
    )


def solution(mesh):
    placed = (
        P("mp", None),
        P("mp", None),
        P("replica", "mp"),
        P("replica", "mp"),
        P("mp"),
        P(("replica", "mp"), None),
    )

    def step(table, accum, lookup_slots, lookup_weights, touched_rows, pooled_grad):
        small = fits_small(mesh, table, lookup_slots, touched_rows, pooled_grad)
        return jax.shard_map(
            per_device_small if small else per_device_general,
            mesh=mesh,
            in_specs=placed,
            out_specs=(P(("replica", "mp"), None), P("mp", None), P("mp", None)),
            check_vma=False,
        )(table, accum, lookup_slots, lookup_weights, touched_rows, pooled_grad)

    return step
```

```python
import functools
import math

import jax
import jax.numpy as jnp
from jax import lax
from jax.experimental import pallas as pl
from jax.experimental.pallas import tpu as pltpu
from jax.sharding import PartitionSpec as P

learn_rate = 0.5
LANES = 128
spots = (0, 3, 1, 2)
MIB = 1 << 20


def build_counts(slots, weights, touch_count):
    bag_count = slots.shape[0]
    block_rows = math.gcd(bag_count, 512)
    columns = jnp.arange(touch_count, dtype=jnp.int32)

    def one_block(block_index):
        slot_block = lax.dynamic_slice_in_dim(slots, block_index * block_rows, block_rows, 0)
        weight_block = lax.dynamic_slice_in_dim(weights, block_index * block_rows, block_rows, 0)
        matches = (slot_block[:, :, None] == columns[None, None, :]).astype(jnp.float32)
        return jnp.sum(matches * weight_block[:, :, None].astype(jnp.float32), axis=1).astype(
            jnp.bfloat16
        )

    blocks = lax.map(one_block, jnp.arange(bag_count // block_rows, dtype=jnp.int32))
    return blocks.reshape(bag_count, touch_count)


def adagrad(row_values, history, gradient):
    history_new = history + gradient * gradient
    return (row_values - learn_rate * gradient / jnp.sqrt(history_new), history_new)


def per_device_general(table, accum, lookup_slots, lookup_weights, touched_rows, pooled_grad):
    touch_count = touched_rows.shape[0]
    feature_dim = table.shape[1]
    bag_local = pooled_grad.shape[0]
    mp_count = lax.axis_size("mp")
    counts = build_counts(lookup_slots, lookup_weights, touch_count)
    row_tile = table[touched_rows]
    tile_low = row_tile.astype(jnp.bfloat16)
    partial_value = jnp.dot(counts, tile_low, preferred_element_type=jnp.float32)
    received = lax.all_to_all(
        partial_value.reshape(mp_count, bag_local, feature_dim),
        "mp",
        split_axis=0,
        concat_axis=0,
        tiled=True,
    )
    pooled = jnp.sum(received, axis=0)
    local_grad = lax.dot_general(
        counts,
        lax.all_gather(pooled_grad, "mp", axis=0, tiled=True),
        (((0,), (0,)), ((), ())),
        preferred_element_type=jnp.float32,
    )
    gradient = lax.psum(local_grad.astype(jnp.bfloat16), "replica").astype(jnp.float32)
    new_rows, new_history = adagrad(row_tile, accum[touched_rows], gradient)
    new_table = table.at[touched_rows].set(new_rows)
    new_accum = accum.at[touched_rows].set(new_history)
    return (pooled, new_table, new_accum)


def vmem():
    return pl.BlockSpec(memory_space=pltpu.VMEM)


def smem():
    return pl.BlockSpec(memory_space=pltpu.SMEM)


def hbm():
    return pl.BlockSpec(memory_space=pltpu.HBM)


def in_hbm(value):
    return pltpu.with_memory_space_constraint(value, pltpu.HBM)


def params(mib):
    return pltpu.CompilerParams(vmem_limit_bytes=mib * MIB)


def pack_kernel(grad_hbm, slots_hbm, weights_hbm, out_ref, slots_ref, weights_ref, slot_rows, weight_rows, sem):
    hots, bags = slots_ref.shape
    rows = grad_hbm.shape[0]
    blocks = bags // LANES
    loads = [
        pltpu.make_async_copy(slots_hbm, slots_ref, sem.at[0]),
        pltpu.make_async_copy(weights_hbm, weights_ref, sem.at[1]),
        pltpu.make_async_copy(grad_hbm, out_ref.at[pl.ds(0, rows), :], sem.at[2]),
    ]
    for load in loads:
        load.start()
    for load in loads:
        load.wait()
    for h in range(hots):
        for j in range(blocks):
            slot_rows[pl.ds(h * blocks + j, 1), :] = slots_ref[pl.ds(h, 1), pl.ds(j * LANES, LANES)]
            weight_rows[pl.ds(h * blocks + j, 1), :] = weights_ref[pl.ds(h, 1), pl.ds(j * LANES, LANES)]
    slot = slot_rows[...]
    code = weight_rows[...] * 64 + lax.shift_right_logical(slot, 8)
    low = jnp.bitwise_and(slot, 255)
    lookups = hots * blocks
    out_ref[pl.ds(rows, lookups), :] = low.astype(jnp.float32).astype(jnp.bfloat16)
    out_ref[pl.ds(rows + lookups, lookups), :] = code.astype(jnp.float32).astype(jnp.bfloat16)


def fill_counts(packed_ref, counts_ref, place, me, hots, low_rows, code_rows):
    touch = counts_ref.shape[0]
    lookups = low_rows.shape[0]
    rows = packed_ref.shape[0] - 2 * lookups
    blocks = lookups // hots
    low_rows[...] = packed_ref[pl.ds(rows, lookups), :].astype(jnp.float32)
    code_rows[...] = packed_ref[pl.ds(rows + lookups, lookups), :].astype(jnp.float32)
    step = min(touch, 256)
    line = lax.broadcasted_iota(jnp.int32, (step, LANES), 0).astype(jnp.float32).astype(jnp.bfloat16)
    zero = jnp.zeros((step, LANES), jnp.bfloat16)

    def one(j, carry):
        distance = jnp.bitwise_xor(j * LANES // rows, me)
        chip = lax.shift_right_logical(distance, 1)
        spot = jnp.where(chip == 3, 1, jnp.where(chip == 0, 0, chip + 1))
        at_column = (
            jnp.bitwise_and(distance, 1) * (counts_ref.shape[1] // 2)
            + lax.shift_right_logical(spot, 1) * (counts_ref.shape[1] // 4)
            + place * (2 * rows)
            + jnp.bitwise_and(spot, 1) * rows
            + j * LANES % rows
        )
        columns = pl.ds(pl.multiple_of(at_column, LANES), LANES)
        lows, highs, weights = [], [], []
        for h in range(hots):
            low = low_rows[pl.ds(h * blocks + j, 1), :]
            code = code_rows[pl.ds(h * blocks + j, 1), :].astype(jnp.int32)
            lows.append(low)
            highs.append(jnp.bitwise_and(code, 63))
            weights.append(lax.shift_right_logical(code, 6).astype(jnp.float32).astype(jnp.bfloat16))
        for k in range(touch // step):
            total = None
            for h in range(hots):
                at = jnp.where(highs[h] == k, lows[h], -1.0).astype(jnp.bfloat16)
                at = jnp.broadcast_to(at, (step, LANES))
                term = jnp.where(at == line, jnp.broadcast_to(weights[h], (step, LANES)), zero)
                total = term if total is None else total + term
            counts_ref[pl.ds(k * step, step), columns] = total
        return carry

    lax.fori_loop(0, blocks, one, 0)


def pooled_kernel(hots, mp, touched_hbm, packed_ref, table_hbm, keep_ref, send_ref, counts_ref,
                  table_vmem, tile, low_rows, code_rows, sum_t, touched_ref, sem):
    touch = touched_ref.shape[0]
    bags = counts_ref.shape[1]
    rows = bags // mp
    blocks = bags // LANES
    me = lax.axis_index("mp")
    loads = [
        pltpu.make_async_copy(touched_hbm, touched_ref, sem.at[0]),
        pltpu.make_async_copy(table_hbm, table_vmem, sem.at[1]),
    ]
    for load in loads:
        load.start()

    fill_counts(packed_ref, counts_ref, 0, me, hots, low_rows, code_rows)
    for load in loads:
        load.wait()

    def gather(i, carry):
        for u in range(128):
            t = i * 128 + u
            tile[pl.ds(t, 1), :] = table_vmem[pl.ds(touched_ref[t], 1), :]
        return carry

    lax.fori_loop(0, touch // 128, gather, 0)
    tile_t = tile[...].T.astype(jnp.bfloat16)
    for half in (0, 1):
        sum_t[:, pl.ds(half * (bags // 2), bags // 2)] = jnp.dot(
            tile_t, counts_ref[:, pl.ds(half * (bags // 2), bags // 2)], preferred_element_type=jnp.float32
        )
    for half, ref in ((0, keep_ref), (bags // 2, send_ref)):
        for c in range(mp // 2):
            ref[c] = sum_t[:, pl.ds(half + spots.index(c) * rows, rows)].T


def join_kernel(rows, *refs):
    out_ref = refs[-1]
    for d, ref in enumerate(refs[:-1]):
        out_ref[pl.ds(d * rows, rows), :] = ref[pl.ds(0, rows), :]


def halves_kernel(rows, keep_ref, got_ref, own_ref, next_ref, out_ref):
    own_ref[...] = keep_ref[0] + got_ref[0]
    next_ref[...] = keep_ref[2] + got_ref[2]
    for place, c in ((0, 1), (1, 3)):
        out_ref[pl.ds(place * rows, rows), :] = (keep_ref[c] + got_ref[c]).astype(jnp.bfloat16)


def fold_kernel(rows, own_ref, next_ref, got_ref, own_out, next_out):
    own_out[...] = own_ref[...] + got_ref[pl.ds(0, rows), :].astype(jnp.float32)
    next_out[...] = (next_ref[...] + got_ref[pl.ds(rows, rows), :].astype(jnp.float32)).astype(next_out.dtype)


def counts_kernel(hots, accum_hbm, *refs):
    peers, (counts_ref, accum_ref, full_ref, low_rows, code_rows, sem) = refs[:-6], refs[-6:]
    full_ref[...] = jnp.zeros_like(full_ref)
    load = pltpu.make_async_copy(accum_hbm, accum_ref, sem)
    load.start()
    me = lax.axis_index("mp")
    for d, ref in enumerate(peers):
        fill_counts(ref, counts_ref, d, me, hots, low_rows, code_rows)

    load.wait()


def merge_kernel(rows, waited_ref, *refs):
    del waited_ref
    blocks, merged_ref = refs[:-1], refs[-1]
    replicas = blocks[0].shape[0] // rows
    for spot, c in enumerate(spots):
        group, p = divmod(spot, 2)
        for d in range(replicas):
            place = spot if d == 0 else len(spots) + (group * (replicas - 1) + d - 1) * 2 + p
            merged_ref[pl.ds(place * rows, rows), :] = blocks[c][pl.ds(d * rows, rows), :]


def hold_kernel(*refs):
    del refs


def hold(values, others, flops=0):
    n = len(values)
    return pl.pallas_call(
        hold_kernel,
        out_shape=[jax.ShapeDtypeStruct(v.shape, v.dtype) for v in values],
        in_specs=[pl.BlockSpec(memory_space=pl.ANY)] * (n + len(others)),
        out_specs=[pl.BlockSpec(memory_space=pl.ANY)] * n,
        input_output_aliases={i: i for i in range(n)},
        compiler_params=params(1),
        cost_estimate=pl.CostEstimate(flops=flops, bytes_accessed=0, transcendentals=0),
        name="hold",
    )(*values, *others)


def pair_kernel(group, rows, near_ref, rest_ref, *refs):
    pair, before, (sum_ref, grads) = refs[:2], refs[2:-2], refs[-2:]
    replicas = pair[0].shape[0] // rows
    for d in range(replicas):
        for p, ref in enumerate(pair):
            grads[pl.ds((2 * d + p) * rows, rows), :] = ref[pl.ds(d * rows, rows), :]
    near, rest = near_ref.shape[1] // 4, rest_ref.shape[1] // 4
    total = jnp.dot(
        near_ref[:, pl.ds(group * near, near)], grads[pl.ds(0, near), :], preferred_element_type=jnp.float32
    ) + jnp.dot(
        rest_ref[:, pl.ds(group * rest, rest)], grads[pl.ds(near, rest), :], preferred_element_type=jnp.float32
    )
    for ref in before:
        total = total + ref[...]
    sum_ref[...] = total


def other_core_sum(near_ref, rest_ref, blocks):
    near, rest = near_ref.shape[1] // 2, rest_ref.shape[1] // 2
    return jnp.dot(
        near_ref[:, pl.ds(near, near)], blocks[pl.ds(0, near), :], preferred_element_type=jnp.float32
    ) + jnp.dot(rest_ref[:, pl.ds(rest, rest)], blocks[pl.ds(near, rest), :], preferred_element_type=jnp.float32)


def spread_kernel(touched_hbm, near_ref, rest_ref, first_ref, blocks, blank_ref, full, summed, touched_ref, sem):
    load = pltpu.make_async_copy(touched_hbm, touched_ref, sem)
    load.start()
    del blank_ref
    summed[...] = first_ref[...] + other_core_sum(near_ref, rest_ref, blocks)
    load.wait()

    def scatter(i, carry):
        for u in range(128):
            t = i * 128 + u
            full[pl.ds(touched_ref[t], 1), :] = summed[pl.ds(t, 1), :]
        return carry

    lax.fori_loop(0, summed.shape[0] // 128, scatter, 0)


def update_kernel(full, table_ref, accum_ref, own_ref, last_ref, new_table_ref, new_accum_ref, pooled_ref,
                  table_vmem, accum_vmem, pooled_vmem, out_sem):
    pooled_vmem[...] = own_ref[...] + last_ref[...].astype(jnp.float32)
    stores = [pltpu.make_async_copy(pooled_vmem, pooled_ref, out_sem.at[2, 0])]
    stores[0].start()
    chunks = 8
    size = table_vmem.shape[0] // chunks
    for c in range(chunks):
        part = pl.ds(c * size, size)
        change = full[part, :]
        history = accum_ref[part, :] + change * change
        table_vmem[part, :] = table_ref[part, :] - learn_rate * change * lax.rsqrt(history)
        accum_vmem[part, :] = history
        for held, out, s in ((table_vmem, new_table_ref, 0), (accum_vmem, new_accum_ref, 1)):
            store = pltpu.make_async_copy(held.at[part, :], out.at[part, :], out_sem.at[s, c])
            store.start()
            stores.append(store)
    for store in stores:
        store.wait()


def per_device_small(table, accum, lookup_slots, lookup_weights, touched_rows, pooled_grad):
    bags, hots = lookup_slots.shape
    touch = touched_rows.shape[0]
    rows, feature = pooled_grad.shape
    table_rows = table.shape[0]
    mp = lax.axis_size("mp")
    replicas = lax.axis_size("replica")
    lookups = hots * (bags // LANES)
    low = jnp.bfloat16

    def swap(value, axis, distance):
        return lax.ppermute(value, axis, [(i, i ^ distance) for i in range(lax.axis_size(axis))])

    packed = pl.pallas_call(
        pack_kernel,
        out_shape=jax.ShapeDtypeStruct((rows + 2 * lookups, LANES), low),
        in_specs=[hbm()] * 3,
        out_specs=vmem(),
        scratch_shapes=[pltpu.VMEM((hots, bags), jnp.int32)] * 2
        + [pltpu.VMEM((lookups, LANES), jnp.int32)] * 2
        + [pltpu.SemaphoreType.DMA((3,))],
        compiler_params=params(8),
        name="pack",
    )(in_hbm(pooled_grad), in_hbm(lookup_slots.T), in_hbm(lookup_weights.T))
    peers = [swap(packed, "replica", d) for d in range(1, replicas)]

    keep, send, near_counts, table_held = pl.pallas_call(
        functools.partial(pooled_kernel, hots, mp),
        out_shape=[
            jax.ShapeDtypeStruct((mp // 2, rows, feature), jnp.float32),
            jax.ShapeDtypeStruct((mp // 2, rows, feature), jnp.float32),
            jax.ShapeDtypeStruct((touch, bags), low),
            jax.ShapeDtypeStruct((table_rows, feature), jnp.float32),
        ],
        in_specs=[hbm(), vmem(), hbm()],
        out_specs=[vmem()] * 4,
        scratch_shapes=[
            pltpu.VMEM((touch, feature), jnp.float32),
            pltpu.VMEM((lookups, LANES), jnp.float32),
            pltpu.VMEM((lookups, LANES), jnp.float32),
            pltpu.VMEM((feature, bags), jnp.float32),
            pltpu.SMEM((touch,), jnp.int32),
            pltpu.SemaphoreType.DMA((2,)),
        ],
        compiler_params=params(20),
        cost_estimate=pl.CostEstimate(flops=2 * touch * bags * feature, bytes_accessed=8 * MIB, transcendentals=0),
        name="pool",
    )(in_hbm(touched_rows), packed, in_hbm(table))

    parts = mp // 2
    got = swap(send, "mp", 1)
    peers = hold(peers, [keep], 1 << 34)
    joined = pl.pallas_call(
        functools.partial(join_kernel, rows),
        out_shape=jax.ShapeDtypeStruct((replicas * rows, feature), low),
        in_specs=[vmem()] * replicas,
        out_specs=vmem(),
        compiler_params=params(8),
        name="join",
    )(packed, *peers)
    far = [swap(joined, "mp", 2 * c) for c in range(1, parts)]

    block = jax.ShapeDtypeStruct((rows, feature), jnp.float32)
    own_sum, next_sum, across = pl.pallas_call(
        functools.partial(halves_kernel, rows),
        out_shape=[block, block, jax.ShapeDtypeStruct((2 * rows, feature), low)],
        in_specs=[vmem()] * 2,
        out_specs=[vmem()] * 3,
        compiler_params=params(8),
        name="halves",
    )(keep, got)
    own_sum, next_sum = pl.pallas_call(
        functools.partial(fold_kernel, rows),
        out_shape=[block, jax.ShapeDtypeStruct((rows, feature), low)],
        in_specs=[vmem()] * 3,
        out_specs=[vmem()] * 2,
        compiler_params=params(8),
        name="fold",
    )(own_sum, next_sum, swap(across, "mp", 2))
    last_sum = swap(next_sum, "mp", 4)

    rest_counts, accum_held, blank = pl.pallas_call(
        functools.partial(counts_kernel, hots),
        out_shape=[
            jax.ShapeDtypeStruct((touch, bags * (replicas - 1)), low),
            jax.ShapeDtypeStruct((table_rows, feature), jnp.float32),
            jax.ShapeDtypeStruct((table_rows, feature), jnp.float32),
        ],
        in_specs=[hbm()] + [vmem()] * (replicas - 1),
        out_specs=[vmem()] * 3,
        scratch_shapes=[pltpu.VMEM((lookups, LANES), jnp.float32)] * 2 + [pltpu.SemaphoreType.DMA],
        compiler_params=params(24),
        cost_estimate=pl.CostEstimate(flops=0, bytes_accessed=0, transcendentals=0),
        name="count",
    )(in_hbm(accum), *peers)

    def pair_sum(group, pair, before, flops):
        return pl.pallas_call(
            functools.partial(pair_kernel, group, rows),
            out_shape=jax.ShapeDtypeStruct((touch, feature), jnp.float32),
            in_specs=[vmem()] * (4 + len(before)),
            out_specs=vmem(),
            scratch_shapes=[pltpu.VMEM((2 * replicas * rows, feature), low)],
            compiler_params=params(16),
            cost_estimate=pl.CostEstimate(flops=flops, bytes_accessed=1, transcendentals=0),
            name="gradient",
        )(near_counts, rest_counts, *pair, *before)

    early = pair_sum(0, [joined, far[2]], [], 0)
    same = pl.pallas_call(
        functools.partial(merge_kernel, rows),
        out_shape=jax.ShapeDtypeStruct((parts * replicas * rows, feature), low),
        in_specs=[pl.BlockSpec(memory_space=pl.ANY)] + [vmem()] * parts,
        out_specs=vmem(),
        compiler_params=params(8),
        name="merge",
    )(early, joined, *far)
    other = swap(same, "mp", 1)

    first = pair_sum(1, far[:2], [early], 1 << 34)

    full = pl.pallas_call(
        spread_kernel,
        out_shape=jax.ShapeDtypeStruct((table_rows, feature), jnp.float32),
        in_specs=[hbm()] + [vmem()] * 5,
        out_specs=vmem(),
        input_output_aliases={5: 0},
        scratch_shapes=[
            pltpu.VMEM((touch, feature), jnp.float32),
            pltpu.SMEM((touch,), jnp.int32),
            pltpu.SemaphoreType.DMA,
        ],
        compiler_params=params(16),
        cost_estimate=pl.CostEstimate(flops=0, bytes_accessed=MIB, transcendentals=0),
        name="spread",
    )(in_hbm(touched_rows), near_counts, rest_counts, first, other, blank)

    new_table, new_accum, pooled = pl.pallas_call(
        update_kernel,
        out_shape=[jax.ShapeDtypeStruct(table.shape, jnp.float32)] * 2 + [block],
        in_specs=[vmem()] * 5,
        out_specs=[hbm()] * 3,
        scratch_shapes=[
            pltpu.VMEM((table_rows, feature), jnp.float32),
            pltpu.VMEM((table_rows, feature), jnp.float32),
            pltpu.VMEM((rows, feature), jnp.float32),
            pltpu.SemaphoreType.DMA((3, 8)),
        ],
        compiler_params=params(16),
        cost_estimate=pl.CostEstimate(flops=0, bytes_accessed=MIB, transcendentals=0),
        name="update",
    )(full, table_held, accum_held, own_sum, last_sum)
    return (pooled, new_table, new_accum)


def fits_small(mesh, table, lookup_slots, touched_rows, pooled_grad):
    mp, replicas = mesh.shape["mp"], mesh.shape["replica"]
    powers = all(n & (n - 1) == 0 for n in (mp, replicas))
    touch = touched_rows.shape[0] // mp
    bags = lookup_slots.shape[0] // replicas
    rows = pooled_grad.shape[0] // (mp * replicas)
    return (
        powers
        and mp == 8
        and replicas == 4
        and lookup_slots.shape[0] * touch <= 4096 * 1024
        and touch % 256 == 0
        and touch <= 16384
        and bags % LANES == 0
        and rows % LANES == 0
        and table.shape[1] == LANES
        and table.shape[0] // mp <= 4096
        and table.shape[0] // mp % 256 == 0
        and touch % LANES == 0
    )


def solution(mesh):
    placed = (
        P("mp", None),
        P("mp", None),
        P("replica", "mp"),
        P("replica", "mp"),
        P("mp"),
        P(("replica", "mp"), None),
    )

    def step(table, accum, lookup_slots, lookup_weights, touched_rows, pooled_grad):
        small = fits_small(mesh, table, lookup_slots, touched_rows, pooled_grad)
        return jax.shard_map(
            per_device_small if small else per_device_general,
            mesh=mesh,
            in_specs=placed,
            out_specs=(P(("replica", "mp"), None), P("mp", None), P("mp", None)),
            check_vma=False,
        )(table, accum, lookup_slots, lookup_weights, touched_rows, pooled_grad)

    return step
```

```python
import functools
import math

import jax
import jax.numpy as jnp
from jax import lax
from jax.experimental import pallas as pl
from jax.experimental.pallas import tpu as pltpu
from jax.sharding import PartitionSpec as P

learn_rate = 0.5
LANES = 128
spots = (0, 3, 1, 2)
MIB = 1 << 20


def build_counts(slots, weights, touch_count):
    bag_count = slots.shape[0]
    block_rows = math.gcd(bag_count, 512)
    columns = jnp.arange(touch_count, dtype=jnp.int32)

    def one_block(block_index):
        slot_block = lax.dynamic_slice_in_dim(slots, block_index * block_rows, block_rows, 0)
        weight_block = lax.dynamic_slice_in_dim(weights, block_index * block_rows, block_rows, 0)
        matches = (slot_block[:, :, None] == columns[None, None, :]).astype(jnp.float32)
        return jnp.sum(matches * weight_block[:, :, None].astype(jnp.float32), axis=1).astype(
            jnp.bfloat16
        )

    blocks = lax.map(one_block, jnp.arange(bag_count // block_rows, dtype=jnp.int32))
    return blocks.reshape(bag_count, touch_count)


def adagrad(row_values, history, gradient):
    history_new = history + gradient * gradient
    return (row_values - learn_rate * gradient / jnp.sqrt(history_new), history_new)


def per_device_general(table, accum, lookup_slots, lookup_weights, touched_rows, pooled_grad):
    touch_count = touched_rows.shape[0]
    feature_dim = table.shape[1]
    bag_local = pooled_grad.shape[0]
    mp_count = lax.axis_size("mp")
    counts = build_counts(lookup_slots, lookup_weights, touch_count)
    row_tile = table[touched_rows]
    tile_low = row_tile.astype(jnp.bfloat16)
    partial_value = jnp.dot(counts, tile_low, preferred_element_type=jnp.float32)
    received = lax.all_to_all(
        partial_value.reshape(mp_count, bag_local, feature_dim),
        "mp",
        split_axis=0,
        concat_axis=0,
        tiled=True,
    )
    pooled = jnp.sum(received, axis=0)
    local_grad = lax.dot_general(
        counts,
        lax.all_gather(pooled_grad, "mp", axis=0, tiled=True),
        (((0,), (0,)), ((), ())),
        preferred_element_type=jnp.float32,
    )
    gradient = lax.psum(local_grad.astype(jnp.bfloat16), "replica").astype(jnp.float32)
    new_rows, new_history = adagrad(row_tile, accum[touched_rows], gradient)
    new_table = table.at[touched_rows].set(new_rows)
    new_accum = accum.at[touched_rows].set(new_history)
    return (pooled, new_table, new_accum)


def vmem():
    return pl.BlockSpec(memory_space=pltpu.VMEM)


def smem():
    return pl.BlockSpec(memory_space=pltpu.SMEM)


def hbm():
    return pl.BlockSpec(memory_space=pltpu.HBM)


def in_hbm(value):
    return pltpu.with_memory_space_constraint(value, pltpu.HBM)


def params(mib):
    return pltpu.CompilerParams(vmem_limit_bytes=mib * MIB)


def pack_kernel(grad_hbm, slots_hbm, weights_hbm, out_ref, slots_ref, weights_ref, slot_rows, weight_rows, sem):
    hots, bags = slots_ref.shape
    rows = grad_hbm.shape[0]
    blocks = bags // LANES
    loads = [
        pltpu.make_async_copy(slots_hbm, slots_ref, sem.at[0]),
        pltpu.make_async_copy(weights_hbm, weights_ref, sem.at[1]),
        pltpu.make_async_copy(grad_hbm, out_ref.at[pl.ds(0, rows), :], sem.at[2]),
    ]
    for load in loads:
        load.start()
    for load in loads:
        load.wait()
    for h in range(hots):
        for j in range(blocks):
            slot_rows[pl.ds(h * blocks + j, 1), :] = slots_ref[pl.ds(h, 1), pl.ds(j * LANES, LANES)]
            weight_rows[pl.ds(h * blocks + j, 1), :] = weights_ref[pl.ds(h, 1), pl.ds(j * LANES, LANES)]
    slot = slot_rows[...]
    code = weight_rows[...] * 64 + lax.shift_right_logical(slot, 8)
    low = jnp.bitwise_and(slot, 255)
    lookups = hots * blocks
    out_ref[pl.ds(rows, lookups), :] = low.astype(jnp.float32).astype(jnp.bfloat16)
    out_ref[pl.ds(rows + lookups, lookups), :] = code.astype(jnp.float32).astype(jnp.bfloat16)


def fill_counts(packed_ref, counts_ref, place, me, hots, low_rows, code_rows):
    touch = counts_ref.shape[0]
    lookups = low_rows.shape[0]
    rows = packed_ref.shape[0] - 2 * lookups
    blocks = lookups // hots
    low_rows[...] = packed_ref[pl.ds(rows, lookups), :].astype(jnp.float32)
    code_rows[...] = packed_ref[pl.ds(rows + lookups, lookups), :].astype(jnp.float32)
    step = min(touch, 256)
    line = lax.broadcasted_iota(jnp.int32, (step, LANES), 0).astype(jnp.float32).astype(jnp.bfloat16)
    zero = jnp.zeros((step, LANES), jnp.bfloat16)

    def one(j, carry):
        distance = jnp.bitwise_xor(j * LANES // rows, me)
        chip = lax.shift_right_logical(distance, 1)
        spot = jnp.where(chip == 3, 1, jnp.where(chip == 0, 0, chip + 1))
        at_column = (
            jnp.bitwise_and(distance, 1) * (counts_ref.shape[1] // 2)
            + lax.shift_right_logical(spot, 1) * (counts_ref.shape[1] // 4)
            + place * (2 * rows)
            + jnp.bitwise_and(spot, 1) * rows
            + j * LANES % rows
        )
        columns = pl.ds(pl.multiple_of(at_column, LANES), LANES)
        lows, highs, weights = [], [], []
        for h in range(hots):
            low = low_rows[pl.ds(h * blocks + j, 1), :]
            code = code_rows[pl.ds(h * blocks + j, 1), :].astype(jnp.int32)
            lows.append(low)
            highs.append(jnp.bitwise_and(code, 63))
            weights.append(lax.shift_right_logical(code, 6).astype(jnp.float32).astype(jnp.bfloat16))
        for k in range(touch // step):
            total = None
            for h in range(hots):
                at = jnp.where(highs[h] == k, lows[h], -1.0).astype(jnp.bfloat16)
                at = jnp.broadcast_to(at, (step, LANES))
                term = jnp.where(at == line, jnp.broadcast_to(weights[h], (step, LANES)), zero)
                total = term if total is None else total + term
            counts_ref[pl.ds(k * step, step), columns] = total
        return carry

    lax.fori_loop(0, blocks, one, 0)


def pooled_kernel(hots, mp, touched_hbm, packed_ref, table_hbm, keep_ref, send_ref, counts_ref,
                  table_vmem, blank_ref, tile, low_rows, code_rows, sum_t, touched_ref, sem):
    touch = touched_ref.shape[0]
    bags = counts_ref.shape[1]
    rows = bags // mp
    blocks = bags // LANES
    me = lax.axis_index("mp")
    loads = [
        pltpu.make_async_copy(touched_hbm, touched_ref, sem.at[0]),
        pltpu.make_async_copy(table_hbm, table_vmem, sem.at[1]),
    ]
    for load in loads:
        load.start()

    fill_counts(packed_ref, counts_ref, 0, me, hots, low_rows, code_rows)
    blank_ref[...] = jnp.zeros_like(blank_ref)
    for load in loads:
        load.wait()

    def gather(i, carry):
        for u in range(128):
            t = i * 128 + u
            tile[pl.ds(t, 1), :] = table_vmem[pl.ds(touched_ref[t], 1), :]
        return carry

    lax.fori_loop(0, touch // 128, gather, 0)
    tile_t = tile[...].T.astype(jnp.bfloat16)
    for half in (0, 1):
        sum_t[:, pl.ds(half * (bags // 2), bags // 2)] = jnp.dot(
            tile_t, counts_ref[:, pl.ds(half * (bags // 2), bags // 2)], preferred_element_type=jnp.float32
        )
    for half, ref in ((0, keep_ref), (bags // 2, send_ref)):
        for c in range(mp // 2):
            ref[c] = sum_t[:, pl.ds(half + spots.index(c) * rows, rows)].T


def join_kernel(rows, *refs):
    out_ref = refs[-1]
    for d, ref in enumerate(refs[:-1]):
        out_ref[pl.ds(d * rows, rows), :] = ref[pl.ds(0, rows), :]


def halves_kernel(rows, keep_ref, got_ref, own_ref, next_ref, out_ref):
    own_ref[...] = keep_ref[0] + got_ref[0]
    next_ref[...] = keep_ref[2] + got_ref[2]
    for place, c in ((0, 1), (1, 3)):
        out_ref[pl.ds(place * rows, rows), :] = (keep_ref[c] + got_ref[c]).astype(jnp.bfloat16)


def fold_kernel(rows, own_ref, next_ref, got_ref, own_out, next_out):
    own_out[...] = own_ref[...] + got_ref[pl.ds(0, rows), :].astype(jnp.float32)
    next_out[...] = (next_ref[...] + got_ref[pl.ds(rows, rows), :].astype(jnp.float32)).astype(next_out.dtype)


def counts_kernel(hots, accum_hbm, *refs):
    peers, (counts_ref, accum_ref, low_rows, code_rows, sem) = refs[:-5], refs[-5:]
    load = pltpu.make_async_copy(accum_hbm, accum_ref, sem)
    load.start()
    me = lax.axis_index("mp")
    for d, ref in enumerate(peers):
        fill_counts(ref, counts_ref, d, me, hots, low_rows, code_rows)

    load.wait()


def merge_kernel(rows, waited_ref, *refs):
    del waited_ref
    blocks, merged_ref = refs[:-1], refs[-1]
    replicas = blocks[0].shape[0] // rows
    for spot, c in enumerate(spots):
        group, p = divmod(spot, 2)
        for d in range(replicas):
            place = spot if d == 0 else len(spots) + (group * (replicas - 1) + d - 1) * 2 + p
            merged_ref[pl.ds(place * rows, rows), :] = blocks[c][pl.ds(d * rows, rows), :]


def hold_kernel(*refs):
    del refs


def hold(values, others, flops=0):
    n = len(values)
    return pl.pallas_call(
        hold_kernel,
        out_shape=[jax.ShapeDtypeStruct(v.shape, v.dtype) for v in values],
        in_specs=[pl.BlockSpec(memory_space=pl.ANY)] * (n + len(others)),
        out_specs=[pl.BlockSpec(memory_space=pl.ANY)] * n,
        input_output_aliases={i: i for i in range(n)},
        compiler_params=params(1),
        cost_estimate=pl.CostEstimate(flops=flops, bytes_accessed=0, transcendentals=0),
        name="hold",
    )(*values, *others)


def pair_kernel(group, rows, near_ref, rest_ref, *refs):
    pair, before, (sum_ref, grads) = refs[:2], refs[2:-2], refs[-2:]
    replicas = pair[0].shape[0] // rows
    for d in range(replicas):
        for p, ref in enumerate(pair):
            grads[pl.ds((2 * d + p) * rows, rows), :] = ref[pl.ds(d * rows, rows), :]
    near, rest = near_ref.shape[1] // 4, rest_ref.shape[1] // 4
    total = jnp.dot(
        near_ref[:, pl.ds(group * near, near)], grads[pl.ds(0, near), :], preferred_element_type=jnp.float32
    ) + jnp.dot(
        rest_ref[:, pl.ds(group * rest, rest)], grads[pl.ds(near, rest), :], preferred_element_type=jnp.float32
    )
    for ref in before:
        total = total + ref[...]
    sum_ref[...] = total


def other_core_sum(near_ref, rest_ref, blocks):
    near, rest = near_ref.shape[1] // 2, rest_ref.shape[1] // 2
    return jnp.dot(
        near_ref[:, pl.ds(near, near)], blocks[pl.ds(0, near), :], preferred_element_type=jnp.float32
    ) + jnp.dot(rest_ref[:, pl.ds(rest, rest)], blocks[pl.ds(near, rest), :], preferred_element_type=jnp.float32)


def spread_kernel(touched_hbm, near_ref, rest_ref, first_ref, blocks, blank_ref, full, summed, touched_ref, sem):
    load = pltpu.make_async_copy(touched_hbm, touched_ref, sem)
    load.start()
    del blank_ref
    summed[...] = first_ref[...] + other_core_sum(near_ref, rest_ref, blocks)
    load.wait()

    def scatter(i, carry):
        for u in range(128):
            t = i * 128 + u
            full[pl.ds(touched_ref[t], 1), :] = summed[pl.ds(t, 1), :]
        return carry

    lax.fori_loop(0, summed.shape[0] // 128, scatter, 0)


def update_kernel(full, table_ref, accum_ref, own_ref, last_ref, new_table_ref, new_accum_ref, pooled_ref,
                  table_vmem, accum_vmem, pooled_vmem, out_sem):
    pooled_vmem[...] = own_ref[...] + last_ref[...].astype(jnp.float32)
    stores = [pltpu.make_async_copy(pooled_vmem, pooled_ref, out_sem.at[2, 0])]
    stores[0].start()
    chunks = 8
    size = table_vmem.shape[0] // chunks
    for c in range(chunks):
        part = pl.ds(c * size, size)
        change = full[part, :]
        history = accum_ref[part, :] + change * change
        table_vmem[part, :] = table_ref[part, :] - learn_rate * change * lax.rsqrt(history)
        accum_vmem[part, :] = history
        for held, out, s in ((table_vmem, new_table_ref, 0), (accum_vmem, new_accum_ref, 1)):
            store = pltpu.make_async_copy(held.at[part, :], out.at[part, :], out_sem.at[s, c])
            store.start()
            stores.append(store)
    for store in stores:
        store.wait()


def per_device_small(table, accum, lookup_slots, lookup_weights, touched_rows, pooled_grad):
    bags, hots = lookup_slots.shape
    touch = touched_rows.shape[0]
    rows, feature = pooled_grad.shape
    table_rows = table.shape[0]
    mp = lax.axis_size("mp")
    replicas = lax.axis_size("replica")
    lookups = hots * (bags // LANES)
    low = jnp.bfloat16

    def swap(value, axis, distance):
        return lax.ppermute(value, axis, [(i, i ^ distance) for i in range(lax.axis_size(axis))])

    packed = pl.pallas_call(
        pack_kernel,
        out_shape=jax.ShapeDtypeStruct((rows + 2 * lookups, LANES), low),
        in_specs=[hbm()] * 3,
        out_specs=vmem(),
        scratch_shapes=[pltpu.VMEM((hots, bags), jnp.int32)] * 2
        + [pltpu.VMEM((lookups, LANES), jnp.int32)] * 2
        + [pltpu.SemaphoreType.DMA((3,))],
        compiler_params=params(8),
        name="pack",
    )(in_hbm(pooled_grad), in_hbm(lookup_slots.T), in_hbm(lookup_weights.T))
    peers = [swap(packed, "replica", d) for d in range(1, replicas)]

    keep, send, near_counts, table_held, blank = pl.pallas_call(
        functools.partial(pooled_kernel, hots, mp),
        out_shape=[
            jax.ShapeDtypeStruct((mp // 2, rows, feature), jnp.float32),
            jax.ShapeDtypeStruct((mp // 2, rows, feature), jnp.float32),
            jax.ShapeDtypeStruct((touch, bags), low),
            jax.ShapeDtypeStruct((table_rows, feature), jnp.float32),
            jax.ShapeDtypeStruct((table_rows, feature), jnp.float32),
        ],
        in_specs=[hbm(), vmem(), hbm()],
        out_specs=[vmem()] * 5,
        scratch_shapes=[
            pltpu.VMEM((touch, feature), jnp.float32),
            pltpu.VMEM((lookups, LANES), jnp.float32),
            pltpu.VMEM((lookups, LANES), jnp.float32),
            pltpu.VMEM((feature, bags), jnp.float32),
            pltpu.SMEM((touch,), jnp.int32),
            pltpu.SemaphoreType.DMA((2,)),
        ],
        compiler_params=params(20),
        cost_estimate=pl.CostEstimate(flops=2 * touch * bags * feature, bytes_accessed=8 * MIB, transcendentals=0),
        name="pool",
    )(in_hbm(touched_rows), packed, in_hbm(table))

    parts = mp // 2
    got = swap(send, "mp", 1)
    peers = hold(peers, [keep], 1 << 34)
    joined = pl.pallas_call(
        functools.partial(join_kernel, rows),
        out_shape=jax.ShapeDtypeStruct((replicas * rows, feature), low),
        in_specs=[vmem()] * replicas,
        out_specs=vmem(),
        compiler_params=params(8),
        name="join",
    )(packed, *peers)
    far = [swap(joined, "mp", 2 * c) for c in range(1, parts)]

    block = jax.ShapeDtypeStruct((rows, feature), jnp.float32)
    own_sum, next_sum, across = pl.pallas_call(
        functools.partial(halves_kernel, rows),
        out_shape=[block, block, jax.ShapeDtypeStruct((2 * rows, feature), low)],
        in_specs=[vmem()] * 2,
        out_specs=[vmem()] * 3,
        compiler_params=params(8),
        name="halves",
    )(keep, got)
    own_sum, next_sum = pl.pallas_call(
        functools.partial(fold_kernel, rows),
        out_shape=[block, jax.ShapeDtypeStruct((rows, feature), low)],
        in_specs=[vmem()] * 3,
        out_specs=[vmem()] * 2,
        compiler_params=params(8),
        name="fold",
    )(own_sum, next_sum, swap(across, "mp", 2))
    last_sum = swap(next_sum, "mp", 4)

    rest_counts, accum_held = pl.pallas_call(
        functools.partial(counts_kernel, hots),
        out_shape=[
            jax.ShapeDtypeStruct((touch, bags * (replicas - 1)), low),
            jax.ShapeDtypeStruct((table_rows, feature), jnp.float32),
        ],
        in_specs=[hbm()] + [vmem()] * (replicas - 1),
        out_specs=[vmem()] * 2,
        scratch_shapes=[pltpu.VMEM((lookups, LANES), jnp.float32)] * 2 + [pltpu.SemaphoreType.DMA],
        compiler_params=params(24),
        cost_estimate=pl.CostEstimate(flops=0, bytes_accessed=0, transcendentals=0),
        name="count",
    )(in_hbm(accum), *peers)

    def pair_sum(group, pair, before, flops):
        return pl.pallas_call(
            functools.partial(pair_kernel, group, rows),
            out_shape=jax.ShapeDtypeStruct((touch, feature), jnp.float32),
            in_specs=[vmem()] * (4 + len(before)),
            out_specs=vmem(),
            scratch_shapes=[pltpu.VMEM((2 * replicas * rows, feature), low)],
            compiler_params=params(16),
            cost_estimate=pl.CostEstimate(flops=flops, bytes_accessed=1, transcendentals=0),
            name="gradient",
        )(near_counts, rest_counts, *pair, *before)

    early = pair_sum(0, [joined, far[2]], [], 0)
    same = pl.pallas_call(
        functools.partial(merge_kernel, rows),
        out_shape=jax.ShapeDtypeStruct((parts * replicas * rows, feature), low),
        in_specs=[pl.BlockSpec(memory_space=pl.ANY)] + [vmem()] * parts,
        out_specs=vmem(),
        compiler_params=params(8),
        name="merge",
    )(early, joined, *far)
    other = swap(same, "mp", 1)

    first = pair_sum(1, far[:2], [early], 1 << 34)

    full = pl.pallas_call(
        spread_kernel,
        out_shape=jax.ShapeDtypeStruct((table_rows, feature), jnp.float32),
        in_specs=[hbm()] + [vmem()] * 5,
        out_specs=vmem(),
        input_output_aliases={5: 0},
        scratch_shapes=[
            pltpu.VMEM((touch, feature), jnp.float32),
            pltpu.SMEM((touch,), jnp.int32),
            pltpu.SemaphoreType.DMA,
        ],
        compiler_params=params(16),
        cost_estimate=pl.CostEstimate(flops=0, bytes_accessed=MIB, transcendentals=0),
        name="spread",
    )(in_hbm(touched_rows), near_counts, rest_counts, first, other, blank)

    new_table, new_accum, pooled = pl.pallas_call(
        update_kernel,
        out_shape=[jax.ShapeDtypeStruct(table.shape, jnp.float32)] * 2 + [block],
        in_specs=[vmem()] * 5,
        out_specs=[hbm()] * 3,
        scratch_shapes=[
            pltpu.VMEM((table_rows, feature), jnp.float32),
            pltpu.VMEM((table_rows, feature), jnp.float32),
            pltpu.VMEM((rows, feature), jnp.float32),
            pltpu.SemaphoreType.DMA((3, 8)),
        ],
        compiler_params=params(16),
        cost_estimate=pl.CostEstimate(flops=0, bytes_accessed=MIB, transcendentals=0),
        name="update",
    )(full, table_held, accum_held, own_sum, last_sum)
    return (pooled, new_table, new_accum)


def fits_small(mesh, table, lookup_slots, touched_rows, pooled_grad):
    mp, replicas = mesh.shape["mp"], mesh.shape["replica"]
    powers = all(n & (n - 1) == 0 for n in (mp, replicas))
    touch = touched_rows.shape[0] // mp
    bags = lookup_slots.shape[0] // replicas
    rows = pooled_grad.shape[0] // (mp * replicas)
    return (
        powers
        and mp == 8
        and replicas == 4
        and lookup_slots.shape[0] * touch <= 4096 * 1024
        and touch % 256 == 0
        and touch <= 16384
        and bags % LANES == 0
        and rows % LANES == 0
        and table.shape[1] == LANES
        and table.shape[0] // mp <= 4096
        and table.shape[0] // mp % 256 == 0
        and touch % LANES == 0
    )


def solution(mesh):
    placed = (
        P("mp", None),
        P("mp", None),
        P("replica", "mp"),
        P("replica", "mp"),
        P("mp"),
        P(("replica", "mp"), None),
    )

    def step(table, accum, lookup_slots, lookup_weights, touched_rows, pooled_grad):
        small = fits_small(mesh, table, lookup_slots, touched_rows, pooled_grad)
        return jax.shard_map(
            per_device_small if small else per_device_general,
            mesh=mesh,
            in_specs=placed,
            out_specs=(P(("replica", "mp"), None), P("mp", None), P("mp", None)),
            check_vma=False,
        )(table, accum, lookup_slots, lookup_weights, touched_rows, pooled_grad)

    return step
```
